128 devices in a mesh: clip: 8 (over x, core), tile: 16 (over z, y).
Axes of the slice: x: 4, y: 4, z: 4, core: 2. Of those that a mesh axis runs over, the one named last changes fastest.
Arguments:
- latents: bfloat16 [32, 32, 2560], P('clip', 'tile'), may hold values from -6 to 6
- tile_route: int32 [32], replicated, may hold values from 0 to 31, as said below
- lengths: int32 [8], replicated, may hold values from 1 to 4, 20 in all
- reward_grad: bfloat16 [8, 4, 32, 160, 384], P('clip', None, 'tile'), may hold values from -6 to 6
- in_kernel: bfloat16 [432, 384], replicated, may hold values from -0.3125 to 0.3125
- in_bias: float32 [384], replicated, may hold values from -4 to 4
- norm_gain: float32 [384], replicated, may hold values from 0.5 to 1.5
- kernel: bfloat16 [10368, 384], replicated, may hold values from -0.0625 to 0.0625
Outputs:
- latent_grad: bfloat16 [32, 32, 2560], P('clip', 'tile')
- weight_grad: float32 [384, 10368], P('tile', 'clip')
The draws below stay inside these ranges and needn't reach their ends.
Inputs may be any that keep to these rules, and one draw needn't show every extreme that they name: A permutation: slot s holds the tile of clip tile_route[s] // 4, frame tile_route[s] % 4; the 4 slots of one index of clip (slots 4 i to 4 i + 3) belong to 4 different clips: slot 4 i + j holds a tile of clip (i + d_j) mod 8, for 4 different shifts d_j that are the same for every i.
All inputs are finite; a program needn't handle non-finite values.
Results may differ from the reference program's by a relative error of at most 0.005.
Values may be sent and summed in bfloat16 or wider, within the bound.
A program may use at most 192 MiB of HBM per device.

```python
import math
import jax
import jax.numpy as jnp
import numpy as np
from jax import lax

C = 384
LAT = 16
F = 4
W = 160
CLIPS = 8
H = 32


def frame_order(key):
    return jax.random.permutation(key, F)


def pick_shifts(key):
    mixed = jax.random.permutation(key, CLIPS).astype(jnp.int32)
    values = jnp.arange(CLIPS, dtype=jnp.int32)
    places = jnp.zeros((CLIPS,), jnp.int32).at[mixed].set(values)
    priority = jnp.where(values == 1, 0, jnp.where(values == CLIPS - 1, 1, jnp.where(values == CLIPS // 2, 2, 3)))
    scores = priority * CLIPS + places
    return jnp.argsort(scores)[:F].astype(jnp.int32)


def draw_tile_route(key, part):
    key = jax.random.fold_in(key, 11)
    shift_key, frame_key = jax.random.split(key)
    shifts = pick_shifts(shift_key)
    owners = jnp.arange(CLIPS, dtype=jnp.int32)[:, None]
    target_clip = (owners + shifts[None, :]) % CLIPS
    orders = jax.vmap(frame_order)(jax.random.split(frame_key, CLIPS)).astype(jnp.int32)
    slot_index = jnp.broadcast_to(jnp.arange(F, dtype=jnp.int32)[None, :], (CLIPS, F))
    frame_pick = orders[target_clip, slot_index]
    return (target_clip * F + frame_pick).reshape(-1).astype(jnp.int32)


def block_scale(own_key, extent, shards, low, high):
    gain = 1.0
    for axis_at, parts in shards:
        steps = jax.random.uniform(jax.random.fold_in(jax.random.fold_in(own_key, 6), axis_at), (parts,), jnp.float32, low / len(shards), high / len(shards))
        gain = gain * jnp.repeat(jnp.exp(steps), extent[axis_at] // parts).reshape((-1,) + (1,) * (len(extent) - 1 - axis_at))
    return gain


def profile(count, total, reach, lean):
    portions = [(1 << 20) // math.isqrt(rank ** lean) + 1 for rank in range(2, count + 1)]
    spare, counts = total - reach - (count - 1), [1] * (count - 1)
    while spare > 0:
        candidates = [i for i in range(count - 1) if counts[i] < reach]
        whole, budget = sum([portions[i] for i in candidates]), spare
        for i in candidates:
            addition = min(reach - counts[i], max(1, budget * portions[i] // whole), spare)
            counts[i] = counts[i] + addition
            spare = spare - addition
    return np.array([reach] + counts)


def ragged_sizes(own_key, count, total, limit, lean):
    if count == 2:
        one = jax.random.randint(own_key, (), max(1, total - limit), min(limit, total - 1) + 1)
        return jnp.stack([one, total - one])
    sizes = jnp.asarray(profile(count, total, limit, lean), jnp.int32)
    pairs = (count - 1) // 2
    source_of, sink = sizes[1:1 + 2 * pairs:2], sizes[2:2 + 2 * pairs:2]
    margin = jnp.minimum(source_of - 1, limit - sink)
    moved = jax.random.randint(jax.random.fold_in(own_key, 1), (pairs,), 0, 1 << 20) % (margin + 1)
    sizes = sizes.at[1:1 + 2 * pairs:2].set(source_of - moved).at[2:2 + 2 * pairs:2].set(sink + moved)
    return sizes[jax.random.permutation(jax.random.fold_in(own_key, 2), count)]


def normal_values(key, extent, scale, reach, shards=(), held_as=jnp.bfloat16):
    entries = scale * jax.random.normal(key, extent, jnp.float32)
    if shards:
        entries = entries * block_scale(key, extent, shards, -0.22, 0.18)
    return jnp.clip(entries, -reach, reach).astype(held_as)


def setup_inputs(seed: int = 0) -> dict:
    key_list = jax.random.split(jax.random.key(seed), 9)
    return {
        "latents": normal_values(key_list[0], (CLIPS * F, H, W * LAT), 1.0, 6.0, ((0, 8), (1, 16))),
        "tile_route": draw_tile_route(jax.random.fold_in(key_list[8], 71), 0),
        "lengths": ragged_sizes(key_list[2], CLIPS, 5 * CLIPS * F // 8, F, 0).astype(jnp.int32),
        "reward_grad": normal_values(key_list[3], (CLIPS, F, H, W, C), 1.0, 6.0, ((0, 8), (2, 16))),
        "in_kernel": normal_values(key_list[4], (27 * LAT, C), (27 * LAT) ** -0.5, 0.3125),
        "in_bias": normal_values(key_list[5], (C,), 1.0, 4.0, (), jnp.float32),
        "norm_gain": jnp.clip(jax.random.uniform(key_list[6], (C,), jnp.float32, 0.5, 1.5), 0.5, 1.5),
        "kernel": normal_values(key_list[7], (27 * C, C), (27 * C) ** -0.5, 0.0625),
    }


EPS = 1e-06

def taps(extended, weights, flipped):
    frame_count = extended.shape[0]
    row_count = extended.shape[1] - 2
    col_count = extended.shape[2]
    channels = extended.shape[3]
    if flipped:
        padded = jnp.pad(extended, ((0, 2), (0, 0), (1, 1), (0, 0)))
        in_width = weights.shape[0] // 27
    else:
        padded = jnp.pad(extended, ((2, 0), (0, 0), (1, 1), (0, 0)))
        in_width = channels
    total = None
    for tap_index in range(27):
        delta_t, delta_y, delta_x = (tap_index // 9, tap_index // 3 % 3, tap_index % 3)
        block_rows = weights[tap_index * in_width:(tap_index + 1) * in_width]
        if flipped:
            window = padded[2 - delta_t:2 - delta_t + frame_count, 2 - delta_y:2 - delta_y + row_count, 2 - delta_x:2 - delta_x + col_count]
            product = lax.dot_general(window.reshape(-1, channels), block_rows, (((1,), (1,)), ((), ())), preferred_element_type=jnp.float32)
        else:
            window = padded[delta_t:delta_t + frame_count, delta_y:delta_y + row_count, delta_x:delta_x + col_count]
            product = jnp.dot(window.reshape(-1, channels), block_rows, preferred_element_type=jnp.float32)
        total = product if total is None else total + product
    return total.reshape(frame_count, row_count, col_count, -1)

def tap_products(extended, cotangent):
    leading = extended.ndim - 4
    padding = [(0, 0)] * leading + [(2, 0), (0, 0), (1, 1), (0, 0)]
    padded = jnp.pad(extended, padding)
    frame_count, row_count, col_count = (cotangent.shape[-4], cotangent.shape[-3], cotangent.shape[-2])
    flat_cot = cotangent.reshape(-1, cotangent.shape[-1])
    products = []
    for tap_index in range(27):
        delta_t, delta_y, delta_x = (tap_index // 9, tap_index // 3 % 3, tap_index % 3)
        window = padded[..., delta_t:delta_t + frame_count, delta_y:delta_y + row_count, delta_x:delta_x + col_count, :]
        products.append(lax.dot_general(window.reshape(-1, padded.shape[-1]), flat_cot, (((0,), (0,)), ((), ())), preferred_element_type=jnp.float32))
    return jnp.concatenate(products, axis=1)

def norm_backward(act_grad, hidden, normed, inv_rms, norm_gain):
    sigmoid_n = jax.nn.sigmoid(normed)
    gained = act_grad * sigmoid_n * (1.0 + normed * (1.0 - sigmoid_n)) * norm_gain
    inner = lax.optimization_barrier(jnp.mean(gained * hidden, axis=-1, keepdims=True))
    return (inv_rms * gained - hidden * inv_rms * inv_rms * inv_rms * inner).astype(jnp.bfloat16)

def pad_rows(field):
    return jnp.pad(field, ((0, 0), (1, 1), (0, 0), (0, 0)))

def reference(latents, tile_route, lengths, reward_grad, in_kernel, in_bias, norm_gain, kernel):
    total_slots = CLIPS * F
    slot_of = jnp.zeros((total_slots,), jnp.int32).at[tile_route].set(jnp.arange(total_slots, dtype=jnp.int32))
    clip_latents = latents[slot_of].reshape(CLIPS, F, H, W, LAT)
    live_mask = (jnp.arange(F, dtype=jnp.int32)[None, :] < lengths[:, None]).astype(jnp.bfloat16)

    def one_clip(carry, inputs):
        latent_clip, live_clip, grad_clip = inputs
        live_cells = live_clip[:, None, None, None]
        masked = latent_clip * live_cells
        hidden = taps(pad_rows(masked), in_kernel, False) + in_bias
        inv_rms = lax.rsqrt(lax.optimization_barrier(jnp.mean(hidden * hidden, axis=-1, keepdims=True)) + EPS)
        normed = hidden * inv_rms * norm_gain
        activated = jax.nn.silu(normed).astype(jnp.bfloat16)
        cotangent = grad_clip * live_cells
        act_grad = taps(pad_rows(cotangent), kernel, True)
        hid_grad = norm_backward(act_grad, hidden, normed, inv_rms, norm_gain)
        lat_grad = (taps(pad_rows(hid_grad), in_kernel, True) * live_cells.astype(jnp.float32)).astype(jnp.bfloat16)
        carry = carry + tap_products(pad_rows(activated), cotangent)
        return (carry, lat_grad)
    zero_carry = jnp.zeros((C, 27 * C), jnp.float32)
    weight_sum, lat_grads = lax.scan(one_clip, zero_carry, (clip_latents, live_mask, reward_grad))
    latent_grad = lat_grads.reshape(total_slots, H, W * LAT)[tile_route]
    weight_grad = weight_sum * (1.0 / math.sqrt(CLIPS * F * H * W))
    return (latent_grad, weight_grad)
```

```python
import math

import jax
import jax.numpy as jnp
from jax import lax
from jax.experimental import pallas as pl
from jax.experimental.pallas import tpu as pltpu
from jax.sharding import PartitionSpec as P

EPS = 1e-06
F, R, W, C, LAT, H, CLIPS = 4, 2, 160, 384, 16, 32, 8
POS = F * R * W
LANES = 256
MESH = pl.DeviceIdType.MESH
BF, F32 = jnp.bfloat16, jnp.float32

WAVES = (
    ((1, 7), ((9, 2), (63, 8)), "zy"),
    ((4,), ((40, 5),), "zy"),
    ((0, 8), ((0, 9),), "yz"),
    ((2, 6), ((20, 7), (60, 3)), "zy"),
    ((3, 5), ((27, 4), (45, 6)), "yz"),
)
OWN = 44


def dot(a, b, ca, cb):
    return lax.dot_general(a, b, (((ca,), (cb,)), ((), ())), preferred_element_type=F32)


def sigmoid(v):
    return 1.0 / (1.0 + jnp.exp(-v))


def kernel(
    route, lengths, lat_in, cot_in, ink, bias, gain, ker_in,
    out_lat, out_wg,
    cotbuf, cot3, kbuf, latg, lat4, s3, xt, hid, act, inv_ref, ag, hg, yt, lg, lgr, latg2,
    gbuf, own, r1, r2, res, q1, qs, q2, fin, x1, xs, x2,
    local_sem, send_sem, recv_sem,
):
    clip, tile = lax.axis_index("clip"), lax.axis_index("tile")
    x, core = clip // 2, clip % 2
    z, y = tile // 4, tile % 4
    me = {"clip": clip, "tile": tile}

    def at(**kw):
        d = {**me, **kw}
        return (d["clip"], d["tile"])

    sib = at(clip=2 * x + 1 - core)
    xp, xm, xo = (at(clip=2 * ((x + k) % 4) + core) for k in (1, 3, 2))
    zp, zm = (at(tile=4 * ((z + k) % 4) + y) for k in (1, 3))
    yp, ym = (at(tile=4 * z + (y + k) % 4) for k in (1, 3))
    tp, tm = (at(tile=(tile + k) % 16) for k in (1, 15))
    peers = (sib, xp, xm, xo, zp, zm, yp, ym, tp, tm)

    copies = []

    def send(src, dst, device):
        n = len(copies)
        cp = pltpu.make_async_remote_copy(
            src_ref=src, dst_ref=dst, send_sem=send_sem.at[n], recv_sem=recv_sem.at[n],
            device_id=device, device_id_type=MESH,
        )
        copies.append(cp)
        cp.start()
        return cp

    load_cot = pltpu.make_async_copy(cot_in.at[0], cotbuf.at[:, 1:3], local_sem.at[0])
    load_cot.start()
    load_ker = pltpu.make_async_copy(ker_in, kbuf, local_sem.at[1])
    load_ker.start()

    barrier = pltpu.get_barrier_semaphore()
    for p in peers:
        pl.semaphore_signal(barrier, inc=1, device_id=p, device_id_type=MESH)
    pl.semaphore_wait(barrier, len(peers))

    lat_x = [send(lat_in, latg.at[clip], d) for d in (xp, xm, xo)]
    lat_s = [send(lat_in, latg.at[clip], sib)]
    halo = [
        send(cot_in.at[0, :, 0], cotbuf.at[:, 3], tm),
        send(cot_in.at[0, :, 1], cotbuf.at[:, 0], tp),
    ]
    latg[clip] = lat_in[...]

    length = lengths[clip]
    live = [jnp.where(f < length, 1.0, 0.0).astype(F32) for f in range(F)]
    top = jnp.where(tile > 0, 1.0, 0.0).astype(F32)
    bottom = jnp.where(tile < 15, 1.0, 0.0).astype(F32)
    edge = (top, 1.0, 1.0, bottom)

    def build_cot(rows):
        col = lax.broadcasted_iota(jnp.int32, (W, C), 0)
        for f in range(F):
            for r in rows:
                v = cotbuf[f, r].astype(F32) * (live[f] * edge[r])
                after = jnp.where(col == W - 1, 0.0, pltpu.roll(v, W - 1, 0))
                before = jnp.where(col == 0, 0.0, pltpu.roll(v, 1, 0))
                cot3[f, r, :, 0:C] = after.astype(BF)
                cot3[f, r, :, C : 2 * C] = v.astype(BF)
                cot3[f, r, :, 2 * C : 3 * C] = before.astype(BF)

    def window(dt, dy):
        return cot3[2 - dt : 4, 2 - dy : 4 - dy].reshape((dt + 2) * R * W, 3 * C)

    def act_grad_part(dt, dy, first):
        t0 = 9 * dt + 3 * dy
        taps = jnp.concatenate([kbuf[(t0 + d) * C : (t0 + d + 1) * C] for d in range(3)], axis=1)
        out = dot(taps, window(dt, dy), 1, 1)
        n = (dt + 2) * R * W
        if first:
            ag[...] = out
        else:
            ag[:, :n] += out

    load_cot.wait()
    build_cot((1, 2))

    for cp in lat_x:
        cp.wait_recv()
    for k in (3, 1, 2):
        src = latg.at[2 * ((x + k) % 4) + core]
        lat_s.append(send(src, src, sib))

    load_ker.wait()
    act_grad_part(2, 1, True)
    for cp in lat_s:
        cp.wait_recv()

    for f in range(F):
        slot = jnp.int32(0)
        for s in range(CLIPS * F):
            slot = jnp.where(route[s] == clip * F + f, s, slot)
        v = latg[slot // F, slot % F].astype(F32) * live[f]
        lat4[f, 1] = v[:LAT].astype(BF)
        lat4[f, 2] = v[LAT:].astype(BF)
    lat_h = [send(lat4.at[:, 1], lat4.at[:, 3], tm), send(lat4.at[:, 2], lat4.at[:, 0], tp)]
    act_grad_part(1, 1, False)
    act_grad_part(0, 1, False)
    for cp in lat_h:
        cp.wait_recv()

    for f in range(F):
        for r in range(4):
            v = lat4[f, r].astype(F32) * edge[r]
            s3[f, r, 0:LAT] = pltpu.roll(v, 1, 1).astype(BF)
            s3[f, r, LAT : 2 * LAT] = v.astype(BF)
            s3[f, r, 2 * LAT :] = pltpu.roll(v, LANES - 1, 1).astype(BF)
    for f in range(F):
        for r in range(R):
            for dt in range(3):
                for dy in range(3):
                    at_rows = slice((3 * dt + dy) * 48, (3 * dt + dy + 1) * 48)
                    at_cols = slice((2 * f + r) * W, (2 * f + r + 1) * W)
                    if f - 2 + dt >= 0:
                        xt[at_rows, at_cols] = s3[f - 2 + dt, r + dy, :, 0:W]
                    else:
                        xt[at_rows, at_cols] = jnp.zeros((48, W), BF)
    hid[...] = dot(ink[...], xt[...], 0, 0) + bias[...]

    def norm_step(n, carry):
        cols = pl.ds(pl.multiple_of(n * 128, 128), 128)
        h = hid[:, cols]
        inv = lax.rsqrt(jnp.mean(h * h, axis=0, keepdims=True) + EPS)
        normed = h * inv * gain[...]
        act[:, cols] = (normed * sigmoid(normed)).astype(BF)
        inv_ref[:, cols] = inv
        return carry

    lax.fori_loop(0, POS // 128, norm_step, 0)

    def weight_part(g, order):
        dt, dy = g // 3, g % 3
        out = dot(act[:, : (dt + 2) * R * W], window(dt, dy), 1, 0)
        for k in range(9):
            v = out[:, 128 * k : 128 * (k + 1)]
            if order == "yz":
                v = jnp.concatenate(
                    [v[24 * (4 * b + a) : 24 * (4 * b + a) + 24] for a in range(4) for b in range(4)], axis=0
                )
            gbuf[9 * g + k] = v.astype(BF)

    def pick(a, b):
        return jnp.where(core == 0, a, b)

    def wave_steps(ranges, order, off):
        total = sum(n for _, n in ranges)
        mine = pl.ds(off, total)
        if order == "zy":
            (a, ap, am), (b, bp, bm) = (z, zp, zm), (y, yp, ym)
        else:
            (a, ap, am), (b, bp, bm) = (y, yp, ym), (z, zp, zm)
        st = {}

        def rows_a(k):
            return 96 * ((a + k) % 4)

        def rows_b(k):
            q = (b + k) % 4
            return pl.multiple_of(48 * (q // 2) + 16 * (q % 2), 16)

        def s0():
            st["c"], at0 = [], off
            for first, n in ranges:
                mirror = 81 - first - n
                src = gbuf.at[pl.ds(pick(mirror, first), n)]
                st["c"].append(send(src, own.at[pl.ds(at0, n)], sib))
                at0 += n

        def s1():
            for cp in st["c"]:
                cp.wait_recv()
            at0 = off
            for first, n in ranges:
                start = pick(first, 81 - first - n)

                def body(k, carry, start=start, at0=at0):
                    own[at0 + k] = (own[at0 + k].astype(F32) + gbuf[start + k].astype(F32)).astype(BF)
                    return carry

                lax.fori_loop(0, n, body, 0)
                at0 += n
            r = pl.multiple_of(rows_a(2), 48)
            st["p1"] = send(own.at[mine, pl.ds(r, 48)], r1.at[mine, 0], ap)
            st["m1"] = send(own.at[mine, pl.ds(pl.multiple_of(r + 48, 48), 48)], r1.at[mine, 1], am)

        def s2():
            for side, k, shift, device in ((0, 1, 0, ap), (1, 3, 48, am)):
                st["pm"[side] + "1"].wait_recv()
                rows = pl.ds(pl.multiple_of(rows_a(k) + shift, 48), 48)

                def body(t, carry, rows=rows, side=side):
                    own[off + t, rows] = (own[off + t, rows].astype(F32) + r1[off + t, side].astype(F32)).astype(BF)
                    return carry

                lax.fori_loop(0, total, body, 0)
                st["pm"[side] + "2"] = send(
                    own.at[mine, pl.ds(pl.multiple_of(rows_a(k), 96), 96)], r2.at[mine, side], device
                )

        def s3_():
            st["p2"].wait_recv()
            st["m2"].wait_recv()
            rows = pl.ds(pl.multiple_of(rows_a(0), 96), 96)

            def body(t, carry):
                i = off + t
                res[i] = (own[i, rows].astype(F32) + r2[i, 0].astype(F32) + r2[i, 1].astype(F32)).astype(BF)
                return carry

            lax.fori_loop(0, total, body, 0)
            r = rows_b(2)
            st["p3"] = send(res.at[mine, pl.ds(r, 16)], q1.at[mine, 0], bp)
            st["m3"] = send(res.at[mine, pl.ds(pl.multiple_of(r + 16, 16), 16)], q1.at[mine, 1], bm)

        def s4():
            for side, k, device in ((0, 1, bp), (1, 3, bm)):
                st["pm"[side] + "3"].wait_recv()
                r = rows_b(k)
                half = pl.ds(pl.multiple_of(r + 16 * side, 16), 16)
                other = pl.ds(pl.multiple_of(r + 16 - 16 * side, 16), 16)

                def body(t, carry, half=half, other=other, side=side):
                    i = off + t
                    qs[i, side, 16 * side : 16 * side + 16] = (
                        res[i, half].astype(F32) + q1[i, side].astype(F32)
                    ).astype(BF)
                    qs[i, side, 16 - 16 * side : 32 - 16 * side] = res[i, other]
                    return carry

                lax.fori_loop(0, total, body, 0)
                st["pm"[side] + "4"] = send(qs.at[mine, side], q2.at[mine, side], device)

        def s5():
            st["p4"].wait_recv()
            st["m4"].wait_recv()
            rows = pl.ds(rows_b(0), 32)
            odd = (b % 2) == 1
            at0 = off
            for first, n in ranges:
                mirror = 81 - first - n
                place = pick(
                    11 * (first // 20) + first % 20, 11 * ((mirror - 10) // 20) + (mirror - 10) % 20
                )

                def body(t, carry, place=place, at0=at0):
                    i = at0 + t
                    v = res[i, rows].astype(F32) + q2[i, 0].astype(F32) + q2[i, 1].astype(F32)
                    v = jnp.where(odd, v[8:], v[:24])
                    fin[place + t] = jnp.concatenate([v, jnp.zeros((8, 128), F32)], axis=0).astype(BF)
                    return carry

                lax.fori_loop(0, n, body, 0)
                at0 += n

        return [s0, s1, s2, s3_, s4, s5]

    in_flight = []

    def advance():
        for steps in list(in_flight):
            steps.pop(0)()
            if not steps:
                in_flight.remove(steps)

    off = 0
    for w, (groups, ranges, order) in enumerate(WAVES):
        if w == 2:
            for cp in halo:
                cp.wait_recv()
            build_cot((0, 3))
        for g in groups:
            weight_part(g, order)
        advance()
        steps = wave_steps(ranges, order, off)
        steps.pop(0)()
        in_flight.append(steps)
        off += sum(n for _, n in ranges)

    act_grad_part(2, 0, False)
    act_grad_part(1, 0, False)
    advance()
    act_grad_part(0, 0, False)
    act_grad_part(2, 2, False)
    advance()
    act_grad_part(1, 2, False)
    act_grad_part(0, 2, False)
    advance()

    def grad_step(n, carry):
        cols = pl.ds(pl.multiple_of(n * 128, 128), 128)
        h, inv = hid[:, cols], inv_ref[:, cols]
        normed = h * inv * gain[...]
        s = sigmoid(normed)
        gained = ag[:, cols] * s * (1.0 + normed * (1.0 - s)) * gain[...]
        inner = jnp.mean(gained * h, axis=0, keepdims=True)
        hg[:, cols] = (inv * gained - h * (inv * inv * inv * inner)).astype(BF)
        return carry

    lax.fori_loop(0, POS // 128, grad_step, 0)
    yt[...] = dot(ink[...], hg[...], 1, 0)

    col = lax.broadcasted_iota(jnp.int32, (LAT, POS), 1) % W
    summed = []
    for g in range(9):
        base = 48 * g
        after = jnp.where(col == W - 1, 0.0, pltpu.roll(yt[base : base + LAT], POS - 1, 1))
        before = jnp.where(col == 0, 0.0, pltpu.roll(yt[base + 2 * LAT : base + 3 * LAT], 1, 1))
        summed.append(yt[base + LAT : base + 2 * LAT] + after + before)
    for f in range(F):
        for r in range(4):
            total = None
            for dt in range(3):
                for dy in range(3):
                    fh, rh = f + 2 - dt, r - dy
                    if fh < F and 0 <= rh < R:
                        p = (2 * fh + rh) * W
                        term = summed[3 * dt + dy][:, p : p + W]
                        total = term if total is None else total + term
            lg[f, r, :, 0:W] = total
            lg[f, r, :, W:] = jnp.zeros((LAT, LANES - W), F32)
    lg_h = [send(lg.at[:, 0], lgr.at[:, 1], tm), send(lg.at[:, 3], lgr.at[:, 0], tp)]
    advance()
    for cp in lg_h:
        cp.wait_recv()
    for f in range(F):
        first = (lg[f, 1] + lgr[f, 0] * top) * live[f]
        second = (lg[f, 2] + lgr[f, 1] * bottom) * live[f]
        latg2[clip, f] = jnp.concatenate([first, second], axis=0).astype(BF)
    back_x = [send(latg2.at[clip], latg2.at[clip], d) for d in (xp, xm, xo)]
    back_s = [send(latg2.at[clip], latg2.at[clip], sib)]
    advance()
    for cp in back_x:
        cp.wait_recv()
    for k in (3, 1, 2):
        src = latg2.at[2 * ((x + k) % 4) + core]
        back_s.append(send(src, src, sib))
    while in_flight:
        advance()

    def win(k):
        return pl.ds(11 * ((x + k) % 4), 11)

    p1 = send(fin.at[win(2), 0:16], x1.at[0], xp)
    m1 = send(fin.at[win(2), 16:32], x1.at[1], xm)
    for cp in back_s:
        cp.wait_recv()
    for j in range(F):
        v = route[clip * F + j]
        out_lat[j] = latg2[v // F, v % F]
    second = []
    for side, k, cp, device in ((0, 1, p1, xp), (1, 3, m1, xm)):
        cp.wait_recv()
        v = fin[win(k)].astype(F32)
        a, b = v[:, 0:16], v[:, 16:32]
        got = x1[side].astype(F32)
        a, b = (a + got, b) if side == 0 else (a, b + got)
        xs[side] = jnp.concatenate([a, b], axis=1).astype(BF)
        second.append(send(xs.at[side], x2.at[side], device))
    for cp in second:
        cp.wait_recv()
    v = fin[win(0)].astype(F32) + x2[0].astype(F32) + x2[1].astype(F32)
    v = v[:, :24] * (1.0 / math.sqrt(CLIPS * F * H * W))
    flat = jnp.concatenate([v[k] for k in range(11)], axis=1)
    out_wg[...] = pltpu.roll(flat, 11 * 128 - 16 * clip, 1)[:, :1296]

    for cp in copies:
        cp.wait_send()


def on_device(latents, tile_route, lengths, reward_grad, in_kernel, in_bias, norm_gain, kernel_):
    lat = latents.reshape(F, R, W, LAT).transpose(0, 1, 3, 2).reshape(F, R * LAT, W)
    lat = jnp.pad(lat, ((0, 0), (0, 0), (0, LANES - W)))
    vmem = pl.BlockSpec(memory_space=pltpu.VMEM)
    smem = pl.BlockSpec(memory_space=pltpu.SMEM)
    hbm = pl.BlockSpec(memory_space=pl.ANY)

    def v(*shape, dtype=BF):
        return pltpu.VMEM(shape, dtype)

    lat_grad, weight_grad = pl.pallas_call(
        kernel,
        out_shape=(
            jax.ShapeDtypeStruct((F, R * LAT, LANES), BF),
            jax.ShapeDtypeStruct((24, 1296), F32),
        ),
        in_specs=[smem, smem, vmem, hbm, vmem, vmem, vmem, hbm],
        out_specs=(vmem, vmem),
        scratch_shapes=[
            v(F, 4, W, C),
            v(F, 4, W, 3 * C),
            v(27 * C, C),
            v(CLIPS, F, R * LAT, LANES),
            v(F, 4, LAT, LANES),
            v(F, 4, 3 * LAT, LANES),
            v(27 * LAT, POS),
            v(C, POS, dtype=F32),
            v(C, POS),
            v(1, POS, dtype=F32),
            v(C, POS, dtype=F32),
            v(C, POS),
            v(27 * LAT, POS, dtype=F32),
            v(F, 4, LAT, LANES, dtype=F32),
            v(F, 2, LAT, LANES, dtype=F32),
            v(CLIPS, F, R * LAT, LANES),
            v(81, C, 128),
            v(OWN, C, 128),
            v(OWN, 2, 48, 128),
            v(OWN, 2, 96, 128),
            v(OWN, 96, 128),
            v(OWN, 2, 16, 128),
            v(OWN, 2, 32, 128),
            v(OWN, 2, 32, 128),
            v(OWN, 32, 128),
            v(2, 11, 16, 128),
            v(2, 11, 32, 128),
            v(2, 11, 32, 128),
            pltpu.SemaphoreType.DMA((2,)),
            pltpu.SemaphoreType.DMA((96,)),
            pltpu.SemaphoreType.DMA((96,)),
        ],
        compiler_params=pltpu.CompilerParams(
            collective_id=0, has_side_effects=True, vmem_limit_bytes=62 * 2**20
        ),
        name="backward",
    )(
        tile_route, lengths, lat, reward_grad, in_kernel,
        in_bias.reshape(C, 1), norm_gain.reshape(C, 1), kernel_,
    )
    lat_grad = lat_grad[:, :, :W].reshape(F, R, LAT, W).transpose(0, 1, 3, 2).reshape(F, R, W * LAT)
    return lat_grad, weight_grad


def solution(mesh):
    return jax.shard_map(
        on_device,
        mesh=mesh,
        in_specs=(
            P("clip", "tile", None),
            P(),
            P(),
            P("clip", None, "tile", None, None),
            P(),
            P(),
            P(),
            P(),
        ),
        out_specs=(P("clip", "tile", None), P("tile", "clip")),
        check_vma=False,
    )
```

```python
import math

import jax
import jax.numpy as jnp
from jax import lax
from jax.experimental import pallas as pl
from jax.experimental.pallas import tpu as pltpu
from jax.sharding import PartitionSpec as P

EPS = 1e-06
F, R, W, C, LAT, H, CLIPS = 4, 2, 160, 384, 16, 32, 8
POS = F * R * W
LANES = 256
MESH = pl.DeviceIdType.MESH
BF, F32 = jnp.bfloat16, jnp.float32

WAVES = (
    ((1, 7), ((9, 2), (63, 8)), "zy"),
    ((4,), ((40, 5),), "zy"),
    ((0, 8), ((0, 9),), "yz"),
    ((2, 6), ((20, 7), (60, 3)), "zy"),
    ((3, 5), ((27, 4), (45, 6)), "yz"),
)
OWN = 44

SCHEDULE = (
    ("G", 1), ("G", 7), (0, 0), ("T", "halo"), ("G", 3), ("G", 5), (4, 0), (0, 1), ("G", 0), ("G", 8), (2, 0),
    ("G", 4), (1, 0), (4, 1), ("G", 2), (0, 2), ("G", 6), (3, 0), (2, 1), (1, 1), ("A", 6), (4, 2), ("A", 3),
    (3, 1), ("A", 0), (2, 2), (0, 3), ("A", 8), (1, 2), ("A", 5), ("A", 2), (3, 2), (4, 3), ("T", "hidden"),
    (1, 3), (2, 3), (3, 3), (0, 4), ("T", "clip"), (1, 4), (4, 4), ("T", "pass"), (3, 4), (2, 4), ("T", "x"),
    ("T", "out"),
)


def dot(a, b, ca, cb):
    return lax.dot_general(a, b, (((ca,), (cb,)), ((), ())), preferred_element_type=F32)


def sigmoid(v):
    return 1.0 / (1.0 + jnp.exp(-v))


def roll(v, shift):
    return pltpu.roll(v, shift % 128, 1) if shift % 128 else v


def pack(tiles, ref):
    rest = None
    for f in range(F):
        ref[f] = tiles[f][:, :128].astype(BF)
        part = roll(tiles[f][:, 128:], 32 * f)
        rest = part if rest is None else rest + part
    ref[F] = rest.astype(BF)


def unpack(ref, slot):
    owner, j = slot // F, slot % F
    rest = ref[owner, F].astype(F32)
    out = rest
    for k in range(1, F):
        out = jnp.where(j == k, roll(rest, -32 * k), out)
    out = jnp.where(lax.broadcasted_iota(jnp.int32, out.shape, 1) < 32, out, 0.0)
    return jnp.concatenate([ref[owner, j].astype(F32), out], axis=1)


def as_column(ref):
    return jnp.broadcast_to(ref[...].reshape(1, C), (8, C)).T[:, :1]


def kernel(
    route, lengths, lat_in, cot_in, ink, bias_in, gain_in, ker_in,
    out_lat, out_wg,
    cotbuf, cot3, kbuf, tr1, tr2, stage, latg, lat4, s3, xt, hid, act, inv_ref, ag, hg, yt, lg, lgr, latg2,
    gbuf, own, r1, r2, res, q, fin, xr,
    local_sem, send_sem, recv_sem,
):
    clip, tile = lax.axis_index("clip"), lax.axis_index("tile")
    x, core = clip // 2, clip % 2
    z, y = tile // 4, tile % 4
    me = {"clip": clip, "tile": tile}

    def at(**kw):
        d = {**me, **kw}
        return (d["clip"], d["tile"])

    sib = at(clip=2 * x + 1 - core)
    xp, xm, xo = (at(clip=2 * ((x + k) % 4) + core) for k in (1, 3, 2))
    zp, zm, zo = (at(tile=4 * ((z + k) % 4) + y) for k in (1, 3, 2))
    yp, ym, yo = (at(tile=4 * z + (y + k) % 4) for k in (1, 3, 2))
    tp, tm = (at(tile=(tile + k) % 16) for k in (1, 15))
    peers = (sib, xp, xm, xo, zp, zm, zo, yp, ym, yo, tp, tm)

    copies = []

    def send(src, dst, device):
        n = len(copies)
        cp = pltpu.make_async_remote_copy(
            src_ref=src, dst_ref=dst, send_sem=send_sem.at[n], recv_sem=recv_sem.at[n],
            device_id=device, device_id_type=MESH,
        )
        copies.append(cp)
        cp.start()
        return cp

    load_cot = pltpu.make_async_copy(cot_in.at[0], cotbuf.at[:, 1:3], local_sem.at[0])
    load_cot.start()
    load_ker = pltpu.make_async_copy(ker_in, kbuf, local_sem.at[1])
    load_ker.start()

    barrier = pltpu.get_barrier_semaphore()
    for p in peers:
        pl.semaphore_signal(barrier, inc=1, device_id=p, device_id_type=MESH)

    lane16 = lax.broadcasted_iota(jnp.int32, (20, 128), 1) // LAT
    flat = jnp.concatenate([lat_in[j].astype(F32) for j in range(F)], axis=0)
    for g in range(20):
        tr1[pl.ds(g, 8, stride=24), :] = flat[:, 128 * g : 128 * (g + 1)]
    tr2[W:] = jnp.zeros((LANES - W, 128), F32)
    for q8 in range(8):
        u = jnp.zeros((20, 128), F32)
        for jr in range(8):
            u = jnp.where(lane16 == jr, roll(tr1[jr * 24 : jr * 24 + 20], LAT * (jr - q8)), u)
        tr2[pl.ds(q8, 20, stride=8), :] = u
    pack(tr2[...].T.reshape(F, R * LAT, LANES), stage)

    pl.semaphore_wait(barrier, len(peers))

    lat_x = [send(stage, latg.at[clip], d) for d in (xp, xm, xo)]
    lat_s = [send(stage, latg.at[clip], sib)]
    halo = [
        send(cot_in.at[0, :, 0], cotbuf.at[:, 3], tm),
        send(cot_in.at[0, :, 1], cotbuf.at[:, 0], tp),
    ]
    latg[clip] = stage[...]

    length = lengths[clip]
    live = [jnp.where(f < length, 1.0, 0.0).astype(F32) for f in range(F)]
    top = jnp.where(tile > 0, 1.0, 0.0).astype(F32)
    bottom = jnp.where(tile < 15, 1.0, 0.0).astype(F32)
    edge = (top, 1.0, 1.0, bottom)

    def build_cot(rows):
        col = lax.broadcasted_iota(jnp.int32, (W, C), 0)
        for f in range(F):
            for r in rows:
                v = cotbuf[f, r].astype(F32) * (live[f] * edge[r])
                after = jnp.where(col == W - 1, 0.0, pltpu.roll(v, W - 1, 0))
                before = jnp.where(col == 0, 0.0, pltpu.roll(v, 1, 0))
                cot3[f, r, :, 0:C] = after.astype(BF)
                cot3[f, r, :, C : 2 * C] = v.astype(BF)
                cot3[f, r, :, 2 * C : 3 * C] = before.astype(BF)

    def window(dt, dy):
        return cot3[2 - dt : 4, 2 - dy : 4 - dy].reshape((dt + 2) * R * W, 3 * C)

    def act_grad_part(dt, dy, first):
        t0 = 9 * dt + 3 * dy
        taps = jnp.concatenate([kbuf[(t0 + d) * C : (t0 + d + 1) * C] for d in range(3)], axis=1)
        out = dot(taps, window(dt, dy), 1, 1)
        n = (dt + 2) * R * W
        if first:
            ag[...] = out
        else:
            ag[:, :n] += out

    load_cot.wait()
    build_cot((1, 2))

    for cp in lat_x:
        cp.wait_recv()
    for k in (3, 1, 2):
        src = latg.at[2 * ((x + k) % 4) + core]
        lat_s.append(send(src, src, sib))

    load_ker.wait()
    act_grad_part(2, 1, True)
    for cp in lat_s:
        cp.wait_recv()

    for f in range(F):
        slot = jnp.int32(0)
        for s in range(CLIPS * F):
            slot = jnp.where(route[s] == clip * F + f, s, slot)
        v = unpack(latg, slot) * live[f]
        lat4[f, 1] = v[:LAT].astype(BF)
        lat4[f, 2] = v[LAT:].astype(BF)
    lat_h = [send(lat4.at[:, 1], lat4.at[:, 3], tm), send(lat4.at[:, 2], lat4.at[:, 0], tp)]
    act_grad_part(1, 1, False)
    act_grad_part(0, 1, False)
    for cp in lat_h:
        cp.wait_recv()

    for f in range(F):
        for r in range(4):
            v = lat4[f, r].astype(F32) * edge[r]
            s3[f, r, 0:LAT] = pltpu.roll(v, 1, 1).astype(BF)
            s3[f, r, LAT : 2 * LAT] = v.astype(BF)
            s3[f, r, 2 * LAT :] = pltpu.roll(v, LANES - 1, 1).astype(BF)
    for f in range(F):
        for r in range(R):
            for dt in range(3):
                for dy in range(3):
                    at_rows = slice((3 * dt + dy) * 48, (3 * dt + dy + 1) * 48)
                    at_cols = slice((2 * f + r) * W, (2 * f + r + 1) * W)
                    if f - 2 + dt >= 0:
                        xt[at_rows, at_cols] = s3[f - 2 + dt, r + dy, :, 0:W]
                    else:
                        xt[at_rows, at_cols] = jnp.zeros((48, W), BF)
    gain = as_column(gain_in)
    hid[...] = dot(ink[...], xt[...], 0, 0) + as_column(bias_in)

    def norm_step(n, carry):
        cols = pl.ds(pl.multiple_of(n * 128, 128), 128)
        h = hid[:, cols]
        inv = lax.rsqrt(jnp.mean(h * h, axis=0, keepdims=True) + EPS)
        normed = h * inv * gain
        act[:, cols] = (normed * sigmoid(normed)).astype(BF)
        inv_ref[:, cols] = inv
        return carry

    lax.fori_loop(0, POS // 128, norm_step, 0)

    def late_rows():
        for cp in halo:
            cp.wait_recv()
        build_cot((0, 3))

    def weight_part(g, order):
        dt, dy = g // 3, g % 3
        out = dot(act[:, : (dt + 2) * R * W], window(dt, dy), 1, 0)
        for k in range(9):
            v = out[:, 128 * k : 128 * (k + 1)]
            if order == "yz":
                v = jnp.concatenate(
                    [v[24 * (4 * b + a) : 24 * (4 * b + a) + 24] for a in range(4) for b in range(4)], axis=0
                )
            gbuf[9 * g + k] = v.astype(BF)

    def pick(a, b):
        return jnp.where(core == 0, a, b)

    def wave_steps(ranges, order, off):
        total = sum(n for _, n in ranges)
        mine = pl.ds(off, total)
        if order == "zy":
            (a, ap, am), (b, bp, bm, bo) = (z, zp, zm), (y, yp, ym, yo)
        else:
            (a, ap, am), (b, bp, bm, bo) = (y, yp, ym), (z, zp, zm, zo)
        st = {}

        def rows_a(k):
            return 96 * ((a + k) % 4)

        def rows_b(k):
            to = (b + k) % 4
            return pl.multiple_of(48 * (to // 2) + 16 * (to % 2), 16)

        def s0():
            st["c"], at0 = [], off
            for first, n in ranges:
                mirror = 81 - first - n
                src = gbuf.at[pl.ds(pick(mirror, first), n)]
                st["c"].append(send(src, own.at[pl.ds(at0, n)], sib))
                at0 += n

        def s1():
            for cp in st["c"]:
                cp.wait_recv()
            at0 = off
            for first, n in ranges:
                start = pick(first, 81 - first - n)

                def body(k, carry, start=start, at0=at0):
                    own[at0 + k] = own[at0 + k] + gbuf[start + k]
                    return carry

                lax.fori_loop(0, n, body, 0)
                at0 += n
            r = pl.multiple_of(rows_a(2), 48)
            st["p1"] = send(own.at[mine, pl.ds(r, 48)], r1.at[mine, 0], ap)
            st["m1"] = send(own.at[mine, pl.ds(pl.multiple_of(r + 48, 48), 48)], r1.at[mine, 1], am)

        def s2():
            for side, k, shift, device in ((0, 1, 0, ap), (1, 3, 48, am)):
                st["pm"[side] + "1"].wait_recv()
                rows = pl.ds(pl.multiple_of(rows_a(k) + shift, 48), 48)

                def body(t, carry, rows=rows, side=side):
                    own[off + t, rows] = own[off + t, rows] + r1[off + t, side]
                    return carry

                lax.fori_loop(0, total, body, 0)
                st["pm"[side] + "2"] = send(
                    own.at[mine, pl.ds(pl.multiple_of(rows_a(k), 96), 96)], r2.at[mine, side], device
                )

        def s3_():
            st["p2"].wait_recv()
            st["m2"].wait_recv()
            rows = pl.ds(pl.multiple_of(rows_a(0), 96), 96)

            def body(t, carry):
                i = off + t
                res[i] = (own[i, rows].astype(F32) + r2[i, 0].astype(F32) + r2[i, 1].astype(F32)).astype(BF)
                return carry

            lax.fori_loop(0, total, body, 0)
            st["q"] = [
                send(res.at[mine, pl.ds(rows_b(k), 32)], q.at[mine, i], device)
                for i, (k, device) in enumerate(((1, bp), (3, bm), (2, bo)))
            ]

        def s4():
            for cp in st["q"]:
                cp.wait_recv()
            rows = pl.ds(rows_b(0), 32)
            odd = (b % 2) == 1
            at0 = off
            for first, n in ranges:
                mirror = 81 - first - n
                place = pick(
                    11 * (first // 20) + first % 20, 11 * ((mirror - 10) // 20) + (mirror - 10) % 20
                )

                def body(t, carry, place=place, at0=at0):
                    i = at0 + t
                    v = res[i, rows].astype(F32) + q[i, 0].astype(F32)
                    v += q[i, 1].astype(F32) + q[i, 2].astype(F32)
                    v = jnp.where(odd, v[8:], v[:24])
                    fin[place + t] = jnp.concatenate([v, jnp.zeros((8, 128), F32)], axis=0).astype(BF)
                    return carry

                lax.fori_loop(0, n, body, 0)
                at0 += n

        return [s0, s1, s2, s3_, s4]

    waves, off = [], 0
    for _, ranges, order in WAVES:
        waves.append(wave_steps(ranges, order, off))
        off += sum(n for _, n in ranges)
    orders = {g: order for groups, _, order in WAVES for g in groups}

    def x_sends():
        def win(k):
            return pl.ds(11 * ((x + k) % 4), 11)

        st["x"] = [send(fin.at[win(k)], xr.at[i], d) for i, (k, d) in enumerate(((1, xp), (3, xm), (2, xo)))]

    def hidden_grad():
        def grad_step(n, carry):
            cols = pl.ds(pl.multiple_of(n * 128, 128), 128)
            h, inv = hid[:, cols], inv_ref[:, cols]
            normed = h * inv * gain
            s = sigmoid(normed)
            gained = ag[:, cols] * s * (1.0 + normed * (1.0 - s)) * gain
            inner = jnp.mean(gained * h, axis=0, keepdims=True)
            hg[:, cols] = (inv * gained - h * (inv * inv * inv * inner)).astype(BF)
            return carry

        lax.fori_loop(0, POS // 128, grad_step, 0)
        yt[...] = dot(ink[...], hg[...], 1, 0)

        col = lax.broadcasted_iota(jnp.int32, (LAT, POS), 1) % W
        summed = []
        for g in range(9):
            base = 48 * g
            after = jnp.where(col == W - 1, 0.0, pltpu.roll(yt[base : base + LAT], POS - 1, 1))
            before = jnp.where(col == 0, 0.0, pltpu.roll(yt[base + 2 * LAT : base + 3 * LAT], 1, 1))
            summed.append(yt[base + LAT : base + 2 * LAT] + after + before)
        for f in range(F):
            for r in range(4):
                total = None
                for dt in range(3):
                    for dy in range(3):
                        fh, rh = f + 2 - dt, r - dy
                        if fh < F and 0 <= rh < R:
                            p = (2 * fh + rh) * W
                            term = summed[3 * dt + dy][:, p : p + W]
                            total = term if total is None else total + term
                lg[f, r, :, 0:W] = total
                lg[f, r, :, W:] = jnp.zeros((LAT, LANES - W), F32)
        st["lg"] = [send(lg.at[:, 0], lgr.at[:, 1], tm), send(lg.at[:, 3], lgr.at[:, 0], tp)]

    def clip_grad():
        for cp in st["lg"]:
            cp.wait_recv()
        tiles = []
        for f in range(F):
            first = (lg[f, 1] + lgr[f, 0] * top) * live[f]
            second = (lg[f, 2] + lgr[f, 1] * bottom) * live[f]
            tiles.append(jnp.concatenate([first, second], axis=0))
        pack(tiles, latg2.at[clip])
        st["bx"] = [send(latg2.at[clip], latg2.at[clip], d) for d in (xp, xm, xo)]
        st["bs"] = [send(latg2.at[clip], latg2.at[clip], sib)]

    def pass_on():
        for cp in st["bx"]:
            cp.wait_recv()
        for k in (3, 1, 2):
            src = latg2.at[2 * ((x + k) % 4) + core]
            st["bs"].append(send(src, src, sib))

    def latent_grad():
        for cp in st["bs"]:
            cp.wait_recv()
        tiles = [unpack(latg2, route[clip * F + j]) for j in range(F)]
        tr2[...] = jnp.concatenate(tiles, axis=0).T
        for jr in range(8):
            u = jnp.zeros((20, 128), F32)
            for q8 in range(8):
                u = jnp.where(lane16 == q8, roll(tr2[pl.ds(q8, 20, stride=8), :], LAT * (q8 - jr)), u)
            tr1[jr * 24 : jr * 24 + 20] = u
        flat = jnp.concatenate([tr1[pl.ds(g, 8, stride=24), :] for g in range(20)], axis=1)
        for j in range(F):
            out_lat[j] = flat[R * j : R * j + R].astype(BF)

    st = {}
    tail = {"halo": late_rows, "hidden": hidden_grad, "clip": clip_grad, "pass": pass_on, "out": latent_grad, "x": x_sends}
    for kind, k in SCHEDULE:
        if kind == "G":
            weight_part(k, orders[k])
        elif kind == "A":
            act_grad_part(k // 3, k % 3, False)
        elif kind == "T":
            tail[k]()
        else:
            waves[kind][k]()

    for cp in st["x"]:
        cp.wait_recv()
    v = fin[pl.ds(11 * x, 11)].astype(F32) + xr[0].astype(F32)
    v += xr[1].astype(F32) + xr[2].astype(F32)
    v = v[:, :24] * (1.0 / math.sqrt(CLIPS * F * H * W))
    flat = jnp.concatenate([v[k] for k in range(11)], axis=1)
    out_wg[...] = pltpu.roll(flat, 11 * 128 - 16 * clip, 1)[:, :1296]

    for cp in copies:
        cp.wait_send()


def on_device(latents, tile_route, lengths, reward_grad, in_kernel, in_bias, norm_gain, kernel_):
    vmem = pl.BlockSpec(memory_space=pltpu.VMEM)
    smem = pl.BlockSpec(memory_space=pltpu.SMEM)
    hbm = pl.BlockSpec(memory_space=pl.ANY)

    def v(*shape, dtype=BF):
        return pltpu.VMEM(shape, dtype)

    return pl.pallas_call(
        kernel,
        out_shape=(
            jax.ShapeDtypeStruct((F, R, W * LAT), BF),
            jax.ShapeDtypeStruct((24, 1296), F32),
        ),
        in_specs=[smem, smem, vmem, hbm, vmem, vmem, vmem, hbm],
        out_specs=(vmem, vmem),
        scratch_shapes=[
            v(F, 4, W, C),
            v(F, 4, W, 3 * C),
            v(27 * C, C),
            v(192, 128, dtype=F32),
            v(LANES, 128, dtype=F32),
            v(F + 1, R * LAT, 128),
            v(CLIPS, F + 1, R * LAT, 128),
            v(F, 4, LAT, LANES),
            v(F, 4, 3 * LAT, LANES),
            v(27 * LAT, POS),
            v(C, POS, dtype=F32),
            v(C, POS),
            v(1, POS, dtype=F32),
            v(C, POS, dtype=F32),
            v(C, POS),
            v(27 * LAT, POS, dtype=F32),
            v(F, 4, LAT, LANES, dtype=F32),
            v(F, 2, LAT, LANES, dtype=F32),
            v(CLIPS, F + 1, R * LAT, 128),
            v(81, C, 128),
            v(OWN, C, 128),
            v(OWN, 2, 48, 128),
            v(OWN, 2, 96, 128),
            v(OWN, 96, 128),
            v(OWN, 3, 32, 128),
            v(OWN, 32, 128),
            v(3, 11, 32, 128),
            pltpu.SemaphoreType.DMA((2,)),
            pltpu.SemaphoreType.DMA((96,)),
            pltpu.SemaphoreType.DMA((96,)),
        ],
        compiler_params=pltpu.CompilerParams(
            collective_id=0, has_side_effects=True, vmem_limit_bytes=62 * 2**20
        ),
        name="backward",
    )(
        tile_route, lengths, latents, reward_grad, in_kernel, in_bias, norm_gain, kernel_,
    )


def solution(mesh):
    return jax.shard_map(
        on_device,
        mesh=mesh,
        in_specs=(
            P("clip", "tile", None),
            P(),
            P(),
            P("clip", None, "tile", None, None),
            P(),
            P(),
            P(),
            P(),
        ),
        out_specs=(P("clip", "tile", None), P("tile", "clip")),
        check_vma=False,
    )
```

```python
import math

import jax
import jax.numpy as jnp
from jax import lax
from jax.experimental import pallas as pl
from jax.experimental.pallas import tpu as pltpu
from jax.sharding import PartitionSpec as P

EPS = 1e-06
F, R, W, C, LAT, H, CLIPS = 4, 2, 160, 384, 16, 32, 8
POS = F * R * W
LANES = 256
MESH = pl.DeviceIdType.MESH
BF, F32 = jnp.bfloat16, jnp.float32

WAVES = (
    ((1, 7), ((9, 2), (63, 8)), "yz"),
    ((4,), ((40, 5),), "yz"),
    ((0, 8), ((0, 9),), "zy"),
    ((2, 6), ((20, 7), (60, 3)), "zy"),
    ((3, 5), ((27, 4), (45, 6)), "yz"),
)
OWN = 44

SCHEDULE = (
    ("G", 4), (1, 0), ("T", "late1"), ("T", "late0"), ("G", 6), (1, 1), ("G", 7), ("G", 5), ("G", 1), (0, 0),
    (1, 2), ("G", 2), (3, 0), ("G", 3), (4, 0), ("G", 0), ("G", 8), (2, 0), (1, 3), (0, 1), (3, 1), (4, 1),
    ("A", 6), (2, 1), (1, 4), ("A", 5), (0, 2), ("A", 3), (3, 2), ("A", 8), (4, 2), (2, 2), ("T", "hidden"),
    (0, 3), (3, 3), (4, 3), (2, 3), ("T", "clip"), (0, 4), (3, 4), (2, 4), (4, 4), ("T", "x"), ("T", "out"),
)


def dot(a, b, ca, cb):
    return lax.dot_general(a, b, (((ca,), (cb,)), ((), ())), preferred_element_type=F32)


def sigmoid(v):
    return 1.0 / (1.0 + jnp.exp(-v))


def roll(v, shift):
    return pltpu.roll(v, shift % 128, 1) if shift % 128 else v


def pack(tiles, ref):
    rest, dtype = None, ref.dtype
    for f in range(F):
        ref[f] = tiles[f][:, :128].astype(dtype)
        part = roll(tiles[f][:, 128:], 32 * f)
        rest = part if rest is None else rest + part
    ref[F] = rest.astype(dtype)


def unpack(ref, slot):
    owner, j = slot // F, slot % F
    rest = ref[owner, F].astype(F32)
    out = rest
    for k in range(1, F):
        out = jnp.where(j == k, roll(rest, -32 * k), out)
    out = jnp.where(lax.broadcasted_iota(jnp.int32, out.shape, 1) < 32, out, 0.0)
    return jnp.concatenate([ref[owner, j].astype(F32), out], axis=1)


def as_column(ref):
    return jnp.broadcast_to(ref[...].reshape(1, C), (8, C)).T[:, :1]


def kernel(
    route, lengths, lat_in, cot_in, ink, bias_in, gain_in, ker_in,
    out_lat, out_wg,
    cotbuf, cot3, kbuf, tr1, tr2, stage, latg, lat4, s3, xt, hid, act, inv_ref, ag, hg, yt, lg, lgs, lgr, latg2,
    gbuf, own, r1, r2, res, q, fin, xr,
    local_sem, send_sem, recv_sem,
):
    clip, tile = lax.axis_index("clip"), lax.axis_index("tile")
    x, core = clip // 2, clip % 2
    z, y = tile // 4, tile % 4
    me = {"clip": clip, "tile": tile}

    def at(**kw):
        d = {**me, **kw}
        return (d["clip"], d["tile"])

    sib = at(clip=2 * x + 1 - core)
    xp, xm, xo = (at(clip=2 * ((x + k) % 4) + core) for k in (1, 3, 2))
    others = tuple(at(clip=2 * ((x + k) % 4) + 1 - core) for k in (1, 3, 2))
    group = (xp, xm, xo) + others + (sib,)
    zp, zm, zo = (at(tile=4 * ((z + k) % 4) + y) for k in (1, 3, 2))
    yp, ym, yo = (at(tile=4 * z + (y + k) % 4) for k in (1, 3, 2))
    tp, tm = (at(tile=(tile + k) % 16) for k in (1, 15))
    peers = (sib, xp, xm, xo, zp, zm, zo, yp, ym, yo, tp, tm) + others

    copies = []

    def send(src, dst, device):
        n = len(copies)
        cp = pltpu.make_async_remote_copy(
            src_ref=src, dst_ref=dst, send_sem=send_sem.at[n], recv_sem=recv_sem.at[n],
            device_id=device, device_id_type=MESH,
        )
        copies.append(cp)
        cp.start()
        return cp

    load_cot = pltpu.make_async_copy(cot_in.at[0], cotbuf.at[:, 1:3], local_sem.at[0])
    load_cot.start()
    load_ker = pltpu.make_async_copy(ker_in, kbuf, local_sem.at[1])
    load_ker.start()

    barrier = pltpu.get_barrier_semaphore()
    for p in peers:
        pl.semaphore_signal(barrier, inc=1, device_id=p, device_id_type=MESH)

    lane16 = lax.broadcasted_iota(jnp.int32, (20, 128), 1) // LAT
    flat = jnp.concatenate([lat_in[j].astype(F32) for j in range(F)], axis=0)
    for g in range(20):
        tr1[pl.ds(g, 8, stride=24), :] = flat[:, 128 * g : 128 * (g + 1)]
    tr2[W:] = jnp.zeros((LANES - W, 128), F32)
    for q8 in range(8):
        u = jnp.zeros((20, 128), F32)
        for jr in range(8):
            u = jnp.where(lane16 == jr, roll(tr1[jr * 24 : jr * 24 + 20], LAT * (jr - q8)), u)
        tr2[pl.ds(q8, 20, stride=8), :] = u
    pack(tr2[...].T.reshape(F, R * LAT, LANES), stage)

    pl.semaphore_wait(barrier, len(peers))

    lat_g = [send(stage, latg.at[clip], d) for d in group]
    parts = (slice(2, 4), slice(1, 2), slice(0, 1))
    halo = [
        [
            send(cot_in.at[0, part, 0], cotbuf.at[part, 3], tm),
            send(cot_in.at[0, part, 1], cotbuf.at[part, 0], tp),
        ]
        for part in parts
    ]
    latg[clip] = stage[...]

    length = lengths[clip]
    live = [jnp.where(f < length, 1.0, 0.0).astype(F32) for f in range(F)]
    top = jnp.where(tile > 0, 1.0, 0.0).astype(F32)
    bottom = jnp.where(tile < 15, 1.0, 0.0).astype(F32)
    edge = (top, 1.0, 1.0, bottom)

    def build_cot(rows, frames):
        col = lax.broadcasted_iota(jnp.int32, (W, C), 0)
        for f in frames:
            for r in rows:
                v = cotbuf[f, r].astype(F32) * (live[f] * edge[r])
                after = jnp.where(col == W - 1, 0.0, pltpu.roll(v, W - 1, 0))
                before = jnp.where(col == 0, 0.0, pltpu.roll(v, 1, 0))
                cot3[f, r, :, 0:C] = after.astype(BF)
                cot3[f, r, :, C : 2 * C] = v.astype(BF)
                cot3[f, r, :, 2 * C : 3 * C] = before.astype(BF)

    def window(dt, dy):
        return cot3[2 - dt : 4, 2 - dy : 4 - dy].reshape((dt + 2) * R * W, 3 * C)

    def act_grad_part(dt, dy, first):
        t0 = 9 * dt + 3 * dy
        taps = jnp.concatenate([kbuf[(t0 + d) * C : (t0 + d + 1) * C] for d in range(3)], axis=1)
        out = dot(taps, window(dt, dy), 1, 1)
        n = (dt + 2) * R * W
        if first:
            ag[...] = out
        else:
            ag[:, :n] += out

    def late_rows(k):
        for cp in halo[k]:
            cp.wait_recv()
        build_cot((0, 3), range(F)[parts[k]])

    load_cot.wait()
    build_cot((1, 2), range(F))

    load_ker.wait()
    act_grad_part(2, 1, True)
    act_grad_part(1, 1, False)
    act_grad_part(0, 1, False)
    for cp in lat_g:
        cp.wait_recv()

    for f in range(F):
        slot = jnp.int32(0)
        for s in range(CLIPS * F):
            slot = jnp.where(route[s] == clip * F + f, s, slot)
        v = unpack(latg, slot) * live[f]
        lat4[f, 1] = v[:LAT].astype(BF)
        lat4[f, 2] = v[LAT:].astype(BF)
    lat_h = [send(lat4.at[:, 1], lat4.at[:, 3], tm), send(lat4.at[:, 2], lat4.at[:, 0], tp)]
    late_rows(0)
    act_grad_part(0, 0, False)
    act_grad_part(0, 2, False)
    for cp in lat_h:
        cp.wait_recv()

    for f in range(F):
        for r in range(4):
            v = lat4[f, r].astype(F32) * edge[r]
            s3[f, r, 0:LAT] = pltpu.roll(v, 1, 1).astype(BF)
            s3[f, r, LAT : 2 * LAT] = v.astype(BF)
            s3[f, r, 2 * LAT :] = pltpu.roll(v, LANES - 1, 1).astype(BF)
    for f in range(F):
        for r in range(R):
            for dt in range(3):
                for dy in range(3):
                    at_rows = slice((3 * dt + dy) * 48, (3 * dt + dy + 1) * 48)
                    at_cols = slice((2 * f + r) * W, (2 * f + r + 1) * W)
                    if f - 2 + dt >= 0:
                        xt[at_rows, at_cols] = s3[f - 2 + dt, r + dy, :, 0:W]
                    else:
                        xt[at_rows, at_cols] = jnp.zeros((48, W), BF)
    gain = as_column(gain_in)
    hid[...] = dot(ink[...], xt[...], 0, 0) + as_column(bias_in)

    def norm_step(n, carry):
        cols = pl.ds(pl.multiple_of(n * 128, 128), 128)
        h = hid[:, cols]
        inv = lax.rsqrt(jnp.mean(h * h, axis=0, keepdims=True) + EPS)
        normed = h * inv * gain
        act[:, cols] = (normed * sigmoid(normed)).astype(BF)
        inv_ref[:, cols] = inv
        return carry

    lax.fori_loop(0, POS // 128, norm_step, 0)

    def weight_part(g, order):
        dt, dy = g // 3, g % 3
        out = dot(act[:, : (dt + 2) * R * W], window(dt, dy), 1, 0)
        for k in range(9):
            v = out[:, 128 * k : 128 * (k + 1)]
            if order == "yz":
                v = jnp.concatenate(
                    [v[24 * (4 * b + a) : 24 * (4 * b + a) + 24] for a in range(4) for b in range(4)], axis=0
                )
            gbuf[9 * g + k] = v.astype(BF)

    def pick(a, b):
        return jnp.where(core == 0, a, b)

    def wave_steps(ranges, order, off):
        total = sum(n for _, n in ranges)
        mine = pl.ds(off, total)
        if order == "zy":
            (a, ap, am), (b, bp, bm, bo) = (z, zp, zm), (y, yp, ym, yo)
        else:
            (a, ap, am), (b, bp, bm, bo) = (y, yp, ym), (z, zp, zm, zo)
        st = {}

        def rows_a(k):
            return 96 * ((a + k) % 4)

        def rows_b(k):
            to = (b + k) % 4
            return pl.multiple_of(48 * (to // 2) + 16 * (to % 2), 16)

        def s0():
            st["c"], at0 = [], off
            for first, n in ranges:
                mirror = 81 - first - n
                src = gbuf.at[pl.ds(pick(mirror, first), n)]
                st["c"].append(send(src, own.at[pl.ds(at0, n)], sib))
                at0 += n

        def s1():
            for cp in st["c"]:
                cp.wait_recv()
            at0 = off
            for first, n in ranges:
                start = pick(first, 81 - first - n)

                def body(k, carry, start=start, at0=at0):
                    own[at0 + k] = own[at0 + k] + gbuf[start + k]
                    return carry

                lax.fori_loop(0, n, body, 0, unroll=True)
                at0 += n
            r = pl.multiple_of(rows_a(2), 48)
            st["p1"] = send(own.at[mine, pl.ds(r, 48)], r1.at[mine, 0], ap)
            st["m1"] = send(own.at[mine, pl.ds(pl.multiple_of(r + 48, 48), 48)], r1.at[mine, 1], am)

        def s2():
            for side, k, shift, device in ((0, 1, 0, ap), (1, 3, 48, am)):
                st["pm"[side] + "1"].wait_recv()
                rows = pl.ds(pl.multiple_of(rows_a(k) + shift, 48), 48)

                def body(t, carry, rows=rows, side=side):
                    own[off + t, rows] = own[off + t, rows] + r1[off + t, side]
                    return carry

                lax.fori_loop(0, total, body, 0, unroll=True)
                st["pm"[side] + "2"] = send(
                    own.at[mine, pl.ds(pl.multiple_of(rows_a(k), 96), 96)], r2.at[mine, side], device
                )

        def s3_():
            st["p2"].wait_recv()
            st["m2"].wait_recv()
            rows = pl.ds(pl.multiple_of(rows_a(0), 96), 96)

            def body(t, carry):
                i = off + t
                res[i] = (own[i, rows].astype(F32) + r2[i, 0].astype(F32) + r2[i, 1].astype(F32)).astype(BF)
                return carry

            lax.fori_loop(0, total, body, 0, unroll=True)
            st["q"] = [
                send(res.at[mine, pl.ds(rows_b(k), 32)], q.at[mine, i], device)
                for i, (k, device) in enumerate(((1, bp), (3, bm), (2, bo)))
            ]

        def s4():
            for cp in st["q"]:
                cp.wait_recv()
            rows = pl.ds(rows_b(0), 32)
            odd = (b % 2) == 1
            at0 = off
            for first, n in ranges:
                mirror = 81 - first - n
                place = pick(
                    11 * (first // 20) + first % 20, 11 * ((mirror - 10) // 20) + (mirror - 10) % 20
                )

                def body(t, carry, place=place, at0=at0):
                    i = at0 + t
                    v = res[i, rows].astype(F32) + q[i, 0].astype(F32)
                    v += q[i, 1].astype(F32) + q[i, 2].astype(F32)
                    v = jnp.where(odd, v[8:], v[:24])
                    fin[place + t] = jnp.concatenate([v, jnp.zeros((8, 128), F32)], axis=0).astype(BF)
                    return carry

                lax.fori_loop(0, n, body, 0, unroll=True)
                at0 += n

        return [s0, s1, s2, s3_, s4]

    waves, off = [], 0
    for _, ranges, order in WAVES:
        waves.append(wave_steps(ranges, order, off))
        off += sum(n for _, n in ranges)
    orders = {g: order for groups, _, order in WAVES for g in groups}

    def x_sends():
        def win(k):
            return pl.ds(11 * ((x + k) % 4), 11)

        st["x"] = [send(fin.at[win(k)], xr.at[i], d) for i, (k, d) in enumerate(((1, xp), (3, xm), (2, xo)))]

    def hidden_grad():
        def grad_step(n, carry):
            cols = pl.ds(pl.multiple_of(n * 128, 128), 128)
            h, inv = hid[:, cols], inv_ref[:, cols]
            normed = h * inv * gain
            s = sigmoid(normed)
            gained = ag[:, cols] * s * (1.0 + normed * (1.0 - s)) * gain
            inner = jnp.mean(gained * h, axis=0, keepdims=True)
            hg[:, cols] = (inv * gained - h * (inv * inv * inv * inner)).astype(BF)
            return carry

        lax.fori_loop(0, POS // 128, grad_step, 0)
        yt[...] = dot(ink[...], hg[...], 1, 0)

        col = lax.broadcasted_iota(jnp.int32, (LAT, POS), 1) % W
        summed = []
        for g in range(9):
            base = 48 * g
            after = jnp.where(col == W - 1, 0.0, pltpu.roll(yt[base : base + LAT], POS - 1, 1))
            before = jnp.where(col == 0, 0.0, pltpu.roll(yt[base + 2 * LAT : base + 3 * LAT], 1, 1))
            summed.append(yt[base + LAT : base + 2 * LAT] + after + before)
        for f in range(F):
            for r in range(4):
                total = None
                for dt in range(3):
                    for dy in range(3):
                        fh, rh = f + 2 - dt, r - dy
                        if fh < F and 0 <= rh < R:
                            p = (2 * fh + rh) * W
                            term = summed[3 * dt + dy][:, p : p + W]
                            total = term if total is None else total + term
                lg[f, r, :, 0:W] = total
                lg[f, r, :, W:] = jnp.zeros((LAT, LANES - W), F32)
        pack([lg[f, 0] for f in range(F)], lgs.at[0])
        pack([lg[f, 3] for f in range(F)], lgs.at[1])
        st["lg"] = [send(lgs.at[0], lgr.at[1], tm), send(lgs.at[1], lgr.at[0], tp)]

    def clip_grad():
        for cp in st["lg"]:
            cp.wait_recv()
        tiles = []
        narrow = lax.broadcasted_iota(jnp.int32, (LAT, 128), 1) < 32
        for f in range(F):
            from_up, from_down = (
                jnp.concatenate(
                    [lgr[k, f], jnp.where(narrow, roll(lgr[k, F], -32 * f), 0.0)], axis=1
                )
                for k in range(2)
            )
            first = (lg[f, 1] + from_up * top) * live[f]
            second = (lg[f, 2] + from_down * bottom) * live[f]
            tiles.append(jnp.concatenate([first, second], axis=0))
        pack(tiles, latg2.at[clip])
        st["back"] = [send(latg2.at[clip], latg2.at[clip], d) for d in group]

    def latent_grad():
        for cp in st["back"]:
            cp.wait_recv()
        tiles = [unpack(latg2, route[clip * F + j]) for j in range(F)]
        tr2[...] = jnp.concatenate(tiles, axis=0).T
        for jr in range(8):
            u = jnp.zeros((20, 128), F32)
            for q8 in range(8):
                u = jnp.where(lane16 == q8, roll(tr2[pl.ds(q8, 20, stride=8), :], LAT * (q8 - jr)), u)
            tr1[jr * 24 : jr * 24 + 20] = u
        flat = jnp.concatenate([tr1[pl.ds(g, 8, stride=24), :] for g in range(20)], axis=1)
        for j in range(F):
            out_lat[j] = flat[R * j : R * j + R].astype(BF)

    st = {}
    tail = {"late1": lambda: late_rows(1), "late0": lambda: late_rows(2), "hidden": hidden_grad, "clip": clip_grad, "out": latent_grad, "x": x_sends}
    for kind, k in SCHEDULE:
        if kind == "G":
            weight_part(k, orders[k])
        elif kind == "A":
            act_grad_part(k // 3, k % 3, False)
        elif kind == "T":
            tail[k]()
        else:
            waves[kind][k]()

    for cp in st["x"]:
        cp.wait_recv()
    v = fin[pl.ds(11 * x, 11)].astype(F32) + xr[0].astype(F32)
    v += xr[1].astype(F32) + xr[2].astype(F32)
    v = v[:, :24] * (1.0 / math.sqrt(CLIPS * F * H * W))
    flat = jnp.concatenate([v[k] for k in range(11)], axis=1)
    out_wg[...] = pltpu.roll(flat, 11 * 128 - 16 * clip, 1)[:, :1296]

    for cp in copies:
        cp.wait_send()


def on_device(latents, tile_route, lengths, reward_grad, in_kernel, in_bias, norm_gain, kernel_):
    vmem = pl.BlockSpec(memory_space=pltpu.VMEM)
    smem = pl.BlockSpec(memory_space=pltpu.SMEM)
    hbm = pl.BlockSpec(memory_space=pl.ANY)

    def v(*shape, dtype=BF):
        return pltpu.VMEM(shape, dtype)

    return pl.pallas_call(
        kernel,
        out_shape=(
            jax.ShapeDtypeStruct((F, R, W * LAT), BF),
            jax.ShapeDtypeStruct((24, 1296), F32),
        ),
        in_specs=[smem, smem, vmem, hbm, vmem, vmem, vmem, hbm],
        out_specs=(vmem, vmem),
        scratch_shapes=[
            v(F, 4, W, C),
            v(F, 4, W, 3 * C),
            v(27 * C, C),
            v(192, 128, dtype=F32),
            v(LANES, 128, dtype=F32),
            v(F + 1, R * LAT, 128),
            v(CLIPS, F + 1, R * LAT, 128),
            v(F, 4, LAT, LANES),
            v(F, 4, 3 * LAT, LANES),
            v(27 * LAT, POS),
            v(C, POS, dtype=F32),
            v(C, POS),
            v(1, POS, dtype=F32),
            v(C, POS, dtype=F32),
            v(C, POS),
            v(27 * LAT, POS, dtype=F32),
            v(F, 4, LAT, LANES, dtype=F32),
            v(2, F + 1, LAT, 128, dtype=F32),
            v(2, F + 1, LAT, 128, dtype=F32),
            v(CLIPS, F + 1, R * LAT, 128),
            v(81, C, 128),
            v(OWN, C, 128),
            v(OWN, 2, 48, 128),
            v(OWN, 2, 96, 128),
            v(OWN, 96, 128),
            v(OWN, 3, 32, 128),
            v(OWN, 32, 128),
            v(3, 11, 32, 128),
            pltpu.SemaphoreType.DMA((2,)),
            pltpu.SemaphoreType.DMA((96,)),
            pltpu.SemaphoreType.DMA((96,)),
        ],
        compiler_params=pltpu.CompilerParams(
            collective_id=0, has_side_effects=True, vmem_limit_bytes=62 * 2**20
        ),
        name="backward",
    )(
        tile_route, lengths, latents, reward_grad, in_kernel, in_bias, norm_gain, kernel_,
    )


def solution(mesh):
    return jax.shard_map(
        on_device,
        mesh=mesh,
        in_specs=(
            P("clip", "tile", None),
            P(),
            P(),
            P("clip", None, "tile", None, None),
            P(),
            P(),
            P(),
            P(),
        ),
        out_specs=(P("clip", "tile", None), P("tile", "clip")),
        check_vma=False,
    )
```

```python
import math

import jax
import jax.numpy as jnp
from jax import lax
from jax.experimental import pallas as pl
from jax.experimental.pallas import tpu as pltpu
from jax.sharding import PartitionSpec as P

EPS = 1e-06
F, R, W, C, LAT, H, CLIPS = 4, 2, 160, 384, 16, 32, 8
POS = F * R * W
LANES = 256
MESH = pl.DeviceIdType.MESH
BF, F32 = jnp.bfloat16, jnp.float32

WAVES = (
    ((1, 7), ((9, 2), (63, 8)), "yz"),
    ((4,), ((40, 5),), "yz"),
    ((0, 8), ((0, 9),), "zy"),
    ((2, 6), ((20, 7), (60, 3)), "zy"),
    ((3, 5), ((27, 4), (45, 6)), "yz"),
)
OWN = 44
FIXED = 96
PAIRS = sum((n + 1) // 2 for _, ranges, _ in WAVES for _, n in ranges)

SCHEDULE = (
    ("G", 7), ("G", 1), (0, 0), ("G", 2), ("T", "late1"), ("T", "late0"), ("G", 6), (3, 0), (0, 1), ("G", 5),
    ("G", 3), (4, 0), ("G", 8), (3, 1), (0, 2), ("G", 0), (2, 0), (4, 1), ("G", 4), (1, 0), ("A", 5), (2, 1),
    (3, 2), ("A", 3), (1, 1), ("A", 6), (0, 3), ("A", 8), (2, 2), (4, 2), ("T", "hidden"), (1, 2), (3, 3),
    (0, 4), (4, 3), ("T", "clip"), (0, 5), (1, 3), (2, 3), (3, 4), (4, 4), (1, 4), (2, 4), ("T", "out"),
    (3, 5), (4, 5), (1, 5), (2, 5),
)


def dot(a, b, ca, cb):
    return lax.dot_general(a, b, (((ca,), (cb,)), ((), ())), preferred_element_type=F32)


def sigmoid(v):
    return 1.0 / (1.0 + jnp.exp(-v))


def roll(v, shift):
    return pltpu.roll(v, shift % 128, 1) if shift % 128 else v


def pack(tiles, ref):
    rest, dtype = None, ref.dtype
    for f in range(F):
        ref[f] = tiles[f][:, :128].astype(dtype)
        part = roll(tiles[f][:, 128:], 32 * f)
        rest = part if rest is None else rest + part
    ref[F] = rest.astype(dtype)


def unpack(ref, slot):
    owner, j = slot // F, slot % F
    rest = ref[owner, F].astype(F32)
    out = rest
    for k in range(1, F):
        out = jnp.where(j == k, roll(rest, -32 * k), out)
    out = jnp.where(lax.broadcasted_iota(jnp.int32, out.shape, 1) < 32, out, 0.0)
    return jnp.concatenate([ref[owner, j].astype(F32), out], axis=1)


def as_column(ref):
    return jnp.broadcast_to(ref[...].reshape(1, C), (8, C)).T[:, :1]


def kernel(
    route, lengths, lat_in, cot_in, ink, bias_in, gain_in, ker_in,
    out_lat, out_wg,
    cotbuf, cot3, kbuf, tr1, tr2, stage, latg, lat4, s3, xt, hid, act, inv_ref, ag, hg, yt, lg, lgs, lgr, latg2,
    gbuf, own, r1, r2, sb, q, fin, fr, outf,
    local_sem, send_sem, recv_sem,
):
    clip, tile = lax.axis_index("clip"), lax.axis_index("tile")
    x, core = clip // 2, clip % 2
    z, y = tile // 4, tile % 4
    me = {"clip": clip, "tile": tile}

    def at(**kw):
        d = {**me, **kw}
        return (d["clip"], d["tile"])

    sib = at(clip=2 * x + 1 - core)
    xp, xm, xo = (at(clip=2 * ((x + k) % 4) + core) for k in (1, 3, 2))
    others = tuple(at(clip=2 * ((x + k) % 4) + 1 - core) for k in (1, 3, 2))
    group = (xp, xm, xo) + others + (sib,)
    zp, zm, zo = (at(tile=4 * ((z + k) % 4) + y) for k in (1, 3, 2))
    yp, ym, yo = (at(tile=4 * z + (y + k) % 4) for k in (1, 3, 2))
    tp, tm = (at(tile=(tile + k) % 16) for k in (1, 15))
    peers = (sib, xp, xm, xo, zp, zm, zo, yp, ym, yo, tp, tm) + others

    copies = []

    def send(src, dst, device):
        n = len(copies)
        assert n < FIXED
        cp = pltpu.make_async_remote_copy(
            src_ref=src, dst_ref=dst, send_sem=send_sem.at[n], recv_sem=recv_sem.at[n],
            device_id=device, device_id_type=MESH,
        )
        copies.append(cp)
        cp.start()
        return cp

    load_cot = pltpu.make_async_copy(cot_in.at[0], cotbuf.at[:, 1:3], local_sem.at[0])
    load_cot.start()
    load_ker = pltpu.make_async_copy(ker_in, kbuf, local_sem.at[1])
    load_ker.start()

    barrier = pltpu.get_barrier_semaphore()
    for p in peers:
        pl.semaphore_signal(barrier, inc=1, device_id=p, device_id_type=MESH)

    lane16 = lax.broadcasted_iota(jnp.int32, (20, 128), 1) // LAT
    flat = jnp.concatenate([lat_in[j].astype(F32) for j in range(F)], axis=0)
    for g in range(20):
        tr1[pl.ds(g, 8, stride=24), :] = flat[:, 128 * g : 128 * (g + 1)]
    tr2[W:] = jnp.zeros((LANES - W, 128), F32)
    for q8 in range(8):
        u = jnp.zeros((20, 128), F32)
        for jr in range(8):
            u = jnp.where(lane16 == jr, roll(tr1[jr * 24 : jr * 24 + 20], LAT * (jr - q8)), u)
        tr2[pl.ds(q8, 20, stride=8), :] = u
    pack(tr2[...].T.reshape(F, R * LAT, LANES), stage)

    pl.semaphore_wait(barrier, len(peers))

    lat_g = [send(stage, latg.at[clip], d) for d in group]
    parts = (slice(2, 4), slice(1, 2), slice(0, 1))
    halo = [
        [
            send(cot_in.at[0, part, 0], cotbuf.at[part, 3], tm),
            send(cot_in.at[0, part, 1], cotbuf.at[part, 0], tp),
        ]
        for part in parts
    ]
    latg[clip] = stage[...]

    length = lengths[clip]
    live = [jnp.where(f < length, 1.0, 0.0).astype(F32) for f in range(F)]
    top = jnp.where(tile > 0, 1.0, 0.0).astype(F32)
    bottom = jnp.where(tile < 15, 1.0, 0.0).astype(F32)
    edge = (top, 1.0, 1.0, bottom)

    def build_cot(rows, frames):
        col = lax.broadcasted_iota(jnp.int32, (W, C), 0)
        for f in frames:
            for r in rows:
                v = cotbuf[f, r].astype(F32) * (live[f] * edge[r])
                after = jnp.where(col == W - 1, 0.0, pltpu.roll(v, W - 1, 0))
                before = jnp.where(col == 0, 0.0, pltpu.roll(v, 1, 0))
                cot3[f, r, :, 0:C] = after.astype(BF)
                cot3[f, r, :, C : 2 * C] = v.astype(BF)
                cot3[f, r, :, 2 * C : 3 * C] = before.astype(BF)

    def window(dt, dy):
        return cot3[2 - dt : 4, 2 - dy : 4 - dy].reshape((dt + 2) * R * W, 3 * C)

    def act_grad_part(dt, dy, first):
        t0 = 9 * dt + 3 * dy
        taps = jnp.concatenate([kbuf[(t0 + d) * C : (t0 + d + 1) * C] for d in range(3)], axis=1)
        out = dot(taps, window(dt, dy), 1, 1)
        n = (dt + 2) * R * W
        if first:
            ag[...] = out
        else:
            ag[:, :n] += out

    def late_rows(k):
        for cp in halo[k]:
            cp.wait_recv()
        build_cot((0, 3), range(F)[parts[k]])

    load_cot.wait()
    build_cot((1, 2), range(F))

    load_ker.wait()
    act_grad_part(2, 1, True)
    act_grad_part(1, 1, False)
    act_grad_part(0, 1, False)
    for cp in lat_g:
        cp.wait_recv()

    for f in range(F):
        slot = jnp.int32(0)
        for s in range(CLIPS * F):
            slot = jnp.where(route[s] == clip * F + f, s, slot)
        v = unpack(latg, slot) * live[f]
        lat4[f, 1] = v[:LAT].astype(BF)
        lat4[f, 2] = v[LAT:].astype(BF)
    lat_h = [send(lat4.at[:, 1], lat4.at[:, 3], tm), send(lat4.at[:, 2], lat4.at[:, 0], tp)]
    late_rows(0)
    act_grad_part(0, 0, False)
    act_grad_part(0, 2, False)
    for cp in lat_h:
        cp.wait_recv()

    for f in range(F):
        for r in range(4):
            v = lat4[f, r].astype(F32) * edge[r]
            s3[f, r, 0:LAT] = pltpu.roll(v, 1, 1).astype(BF)
            s3[f, r, LAT : 2 * LAT] = v.astype(BF)
            s3[f, r, 2 * LAT :] = pltpu.roll(v, LANES - 1, 1).astype(BF)
    for f in range(F):
        for r in range(R):
            for dt in range(3):
                for dy in range(3):
                    at_rows = slice((3 * dt + dy) * 48, (3 * dt + dy + 1) * 48)
                    at_cols = slice((2 * f + r) * W, (2 * f + r + 1) * W)
                    if f - 2 + dt >= 0:
                        xt[at_rows, at_cols] = s3[f - 2 + dt, r + dy, :, 0:W]
                    else:
                        xt[at_rows, at_cols] = jnp.zeros((48, W), BF)
    gain = as_column(gain_in)
    hid[...] = dot(ink[...], xt[...], 0, 0) + as_column(bias_in)

    def norm_step(n, carry):
        cols = pl.ds(pl.multiple_of(n * 128, 128), 128)
        h = hid[:, cols]
        inv = lax.rsqrt(jnp.mean(h * h, axis=0, keepdims=True) + EPS)
        normed = h * inv * gain
        act[:, cols] = (normed * sigmoid(normed)).astype(BF)
        inv_ref[:, cols] = inv
        return carry

    lax.fori_loop(0, POS // 128, norm_step, 0)

    def weight_part(g, order):
        dt, dy = g // 3, g % 3
        out = dot(act[:, : (dt + 2) * R * W], window(dt, dy), 1, 0)
        for k in range(9):
            v = out[:, 128 * k : 128 * (k + 1)]
            if order == "yz":
                v = jnp.concatenate(
                    [v[24 * (4 * b + a) : 24 * (4 * b + a) + 24] for a in range(4) for b in range(4)], axis=0
                )
            gbuf[9 * g + k] = v.astype(BF)

    def pick(a, b):
        return jnp.where(core == 0, a, b)

    to_owner = []

    def wave_steps(ranges, order, off, poff):
        total = sum(n for _, n in ranges)
        mine = pl.ds(off, total)
        if order == "zy":
            (a, ap, am), (b, bp, bm, bo) = (z, zp, zm), (y, yp, ym, yo)
        else:
            (a, ap, am), (b, bp, bm, bo) = (y, yp, ym), (z, zp, zm, zo)
        st = {}

        def rows_a(k):
            return 96 * ((a + k) % 4)

        def s0():
            st["c"], at0 = [], off
            for first, n in ranges:
                mirror = 81 - first - n
                src = gbuf.at[pl.ds(pick(mirror, first), n)]
                st["c"].append(send(src, own.at[pl.ds(at0, n)], sib))
                at0 += n

        def s1():
            for cp in st["c"]:
                cp.wait_recv()
            at0 = off
            for first, n in ranges:
                start = pick(first, 81 - first - n)

                def body(k, carry, start=start, at0=at0):
                    own[at0 + k] = own[at0 + k] + gbuf[start + k]
                    return carry

                lax.fori_loop(0, n, body, 0, unroll=True)
                at0 += n
            r = pl.multiple_of(rows_a(2), 48)
            st["p1"] = send(own.at[mine, pl.ds(r, 48)], r1.at[mine, 0], ap)
            st["m1"] = send(own.at[mine, pl.ds(pl.multiple_of(r + 48, 48), 48)], r1.at[mine, 1], am)

        def s2():
            for side, k, shift, device in ((0, 1, 0, ap), (1, 3, 48, am)):
                st["pm"[side] + "1"].wait_recv()
                rows = pl.ds(pl.multiple_of(rows_a(k) + shift, 48), 48)

                def body(t, carry, rows=rows, side=side):
                    own[off + t, rows] = own[off + t, rows] + r1[off + t, side]
                    return carry

                lax.fori_loop(0, total, body, 0, unroll=True)
                st["pm"[side] + "2"] = send(
                    own.at[mine, pl.ds(pl.multiple_of(rows_a(k), 96), 96)], r2.at[mine, side], device
                )

        def s3_():
            st["p2"].wait_recv()
            st["m2"].wait_recv()
            rows = pl.ds(pl.multiple_of(rows_a(0), 96), 96)

            def block(i):
                return own[i, rows].astype(F32) + r2[i, 0].astype(F32) + r2[i, 1].astype(F32)

            at0, p = off, poff
            for _, n in ranges:
                for i in range(at0, at0 + n, 2):
                    one = block(i)
                    two = block(i + 1) if i + 1 < at0 + n else jnp.zeros_like(one)
                    for to in range(4):
                        part = slice(24 * to, 24 * to + 24)
                        sb[to, p] = jnp.concatenate([one[part], two[part]], axis=0).astype(BF)
                    p += 1
                at0 += n
            pairs = pl.ds(poff, p - poff)
            st["q"] = [
                send(sb.at[(b + k) % 4, pairs], q.at[i, pairs], device)
                for i, (k, device) in enumerate(((1, bp), (3, bm), (2, bo)))
            ]

        def s4():
            for cp in st["q"]:
                cp.wait_recv()
            p, st["owner"] = poff, []
            for first, n in ranges:
                count = (n + 1) // 2
                for i in range(p, p + count):
                    v = sb[b, i].astype(F32) + q[0, i].astype(F32)
                    fin[i] = (v + q[1, i].astype(F32) + q[2, i].astype(F32)).astype(BF)
                mirror = 81 - first - n
                owner = pick(first // 20, (mirror - 10) // 20)
                base = FIXED + 4 * len(to_owner)
                cp = pltpu.make_async_remote_copy(
                    src_ref=fin.at[pl.ds(p, count)], dst_ref=fr.at[x, pl.ds(p, count)],
                    send_sem=send_sem.at[base], recv_sem=recv_sem.at[base + x],
                    device_id=at(clip=2 * owner + core), device_id_type=MESH,
                )
                to_owner.append((owner, cp))
                st["owner"].append((owner, base, p, n, pick(first % 20, (mirror - 10) % 20)))
                pl.when(owner != x)(cp.start)
                p += count

        def s5():
            for owner, base, p, n, place in st["owner"]:

                @pl.when(owner == x)
                def _(base=base, p=p, n=n, place=place):
                    count = (n + 1) // 2
                    others_x = [(x + k) % 4 for k in (1, 3, 2)]
                    for k in others_x:
                        pltpu.make_async_remote_copy(
                            src_ref=fin.at[pl.ds(p, count)], dst_ref=fr.at[k, pl.ds(p, count)],
                            send_sem=send_sem.at[base], recv_sem=recv_sem.at[base + k],
                            device_id=xp, device_id_type=MESH,
                        ).wait_recv()
                    for i in range(count):
                        v = fin[p + i].astype(F32)
                        for k in others_x:
                            v += fr[k, p + i].astype(F32)
                        outf[place + 2 * i] = v[:24]
                        if 2 * i + 1 < n:
                            outf[place + 2 * i + 1] = v[24:]

        return [s0, s1, s2, s3_, s4, s5]

    waves, off, poff = [], 0, 0
    for _, ranges, order in WAVES:
        waves.append(wave_steps(ranges, order, off, poff))
        off += sum(n for _, n in ranges)
        poff += sum((n + 1) // 2 for _, n in ranges)
    orders = {g: order for groups, _, order in WAVES for g in groups}

    def hidden_grad():
        def grad_step(n, carry):
            cols = pl.ds(pl.multiple_of(n * 128, 128), 128)
            h, inv = hid[:, cols], inv_ref[:, cols]
            normed = h * inv * gain
            s = sigmoid(normed)
            gained = ag[:, cols] * s * (1.0 + normed * (1.0 - s)) * gain
            inner = jnp.mean(gained * h, axis=0, keepdims=True)
            hg[:, cols] = (inv * gained - h * (inv * inv * inv * inner)).astype(BF)
            return carry

        lax.fori_loop(0, POS // 128, grad_step, 0)
        yt[...] = dot(ink[...], hg[...], 1, 0)

        col = lax.broadcasted_iota(jnp.int32, (LAT, POS), 1) % W
        summed = []
        for g in range(9):
            base = 48 * g
            after = jnp.where(col == W - 1, 0.0, pltpu.roll(yt[base : base + LAT], POS - 1, 1))
            before = jnp.where(col == 0, 0.0, pltpu.roll(yt[base + 2 * LAT : base + 3 * LAT], 1, 1))
            summed.append(yt[base + LAT : base + 2 * LAT] + after + before)
        for f in range(F):
            for r in range(4):
                total = None
                for dt in range(3):
                    for dy in range(3):
                        fh, rh = f + 2 - dt, r - dy
                        if fh < F and 0 <= rh < R:
                            p = (2 * fh + rh) * W
                            term = summed[3 * dt + dy][:, p : p + W]
                            total = term if total is None else total + term
                lg[f, r, :, 0:W] = total
                lg[f, r, :, W:] = jnp.zeros((LAT, LANES - W), F32)
        pack([lg[f, 0] for f in range(F)], lgs.at[0])
        pack([lg[f, 3] for f in range(F)], lgs.at[1])
        st["lg"] = [send(lgs.at[0], lgr.at[1], tm), send(lgs.at[1], lgr.at[0], tp)]

    def clip_grad():
        for cp in st["lg"]:
            cp.wait_recv()
        tiles = []
        narrow = lax.broadcasted_iota(jnp.int32, (LAT, 128), 1) < 32
        for f in range(F):
            from_up, from_down = (
                jnp.concatenate(
                    [lgr[k, f], jnp.where(narrow, roll(lgr[k, F], -32 * f), 0.0)], axis=1
                )
                for k in range(2)
            )
            first = (lg[f, 1] + from_up * top) * live[f]
            second = (lg[f, 2] + from_down * bottom) * live[f]
            tiles.append(jnp.concatenate([first, second], axis=0))
        pack(tiles, latg2.at[clip])
        st["back"] = [send(latg2.at[clip], latg2.at[clip], d) for d in group]

    def latent_grad():
        for cp in st["back"]:
            cp.wait_recv()
        tiles = [unpack(latg2, route[clip * F + j]) for j in range(F)]
        tr2[...] = jnp.concatenate(tiles, axis=0).T
        for jr in range(8):
            u = jnp.zeros((20, 128), F32)
            for q8 in range(8):
                u = jnp.where(lane16 == q8, roll(tr2[pl.ds(q8, 20, stride=8), :], LAT * (q8 - jr)), u)
            tr1[jr * 24 : jr * 24 + 20] = u
        flat = jnp.concatenate([tr1[pl.ds(g, 8, stride=24), :] for g in range(20)], axis=1)
        for j in range(F):
            out_lat[j] = flat[R * j : R * j + R].astype(BF)

    st = {}
    tail = {"late1": lambda: late_rows(1), "late0": lambda: late_rows(2), "hidden": hidden_grad, "clip": clip_grad, "out": latent_grad}
    for kind, k in SCHEDULE:
        if kind == "G":
            weight_part(k, orders[k])
        elif kind == "A":
            act_grad_part(k // 3, k % 3, False)
        elif kind == "T":
            tail[k]()
        else:
            waves[kind][k]()

    scale = 1.0 / math.sqrt(CLIPS * F * H * W)
    flat = jnp.concatenate([outf[k] * scale for k in range(11)], axis=1)
    out_wg[...] = pltpu.roll(flat, 11 * 128 - 16 * clip, 1)[:, :1296]

    for cp in copies:
        cp.wait_send()
    for owner, cp in to_owner:
        pl.when(owner != x)(cp.wait_send)


def on_device(latents, tile_route, lengths, reward_grad, in_kernel, in_bias, norm_gain, kernel_):
    vmem = pl.BlockSpec(memory_space=pltpu.VMEM)
    smem = pl.BlockSpec(memory_space=pltpu.SMEM)
    hbm = pl.BlockSpec(memory_space=pl.ANY)

    def v(*shape, dtype=BF):
        return pltpu.VMEM(shape, dtype)

    return pl.pallas_call(
        kernel,
        out_shape=(
            jax.ShapeDtypeStruct((F, R, W * LAT), BF),
            jax.ShapeDtypeStruct((24, 1296), F32),
        ),
        in_specs=[smem, smem, vmem, hbm, vmem, vmem, vmem, hbm],
        out_specs=(vmem, vmem),
        scratch_shapes=[
            v(F, 4, W, C),
            v(F, 4, W, 3 * C),
            v(27 * C, C),
            v(192, 128, dtype=F32),
            v(LANES, 128, dtype=F32),
            v(F + 1, R * LAT, 128),
            v(CLIPS, F + 1, R * LAT, 128),
            v(F, 4, LAT, LANES),
            v(F, 4, 3 * LAT, LANES),
            v(27 * LAT, POS),
            v(C, POS, dtype=F32),
            v(C, POS),
            v(1, POS, dtype=F32),
            v(C, POS, dtype=F32),
            v(C, POS),
            v(27 * LAT, POS, dtype=F32),
            v(F, 4, LAT, LANES, dtype=F32),
            v(2, F + 1, LAT, 128, dtype=F32),
            v(2, F + 1, LAT, 128, dtype=F32),
            v(CLIPS, F + 1, R * LAT, 128),
            v(81, C, 128),
            v(OWN, C, 128),
            v(OWN, 2, 48, 128),
            v(OWN, 2, 96, 128),
            v(4, PAIRS, 48, 128),
            v(3, PAIRS, 48, 128),
            v(PAIRS, 48, 128),
            v(4, PAIRS, 48, 128),
            v(11, 24, 128, dtype=F32),
            pltpu.SemaphoreType.DMA((2,)),
            pltpu.SemaphoreType.DMA((FIXED + 36,)),
            pltpu.SemaphoreType.DMA((FIXED + 36,)),
        ],
        compiler_params=pltpu.CompilerParams(
            collective_id=0, has_side_effects=True, vmem_limit_bytes=62 * 2**20
        ),
        name="backward",
    )(
        tile_route, lengths, latents, reward_grad, in_kernel, in_bias, norm_gain, kernel_,
    )


def solution(mesh):
    return jax.shard_map(
        on_device,
        mesh=mesh,
        in_specs=(
            P("clip", "tile", None),
            P(),
            P(),
            P("clip", None, "tile", None, None),
            P(),
            P(),
            P(),
            P(),
        ),
        out_specs=(P("clip", "tile", None), P("tile", "clip")),
        check_vma=False,
    )
```

```python
import math

import jax
import jax.numpy as jnp
from jax import lax
from jax.experimental import pallas as pl
from jax.experimental.pallas import tpu as pltpu
from jax.sharding import PartitionSpec as P

EPS = 1e-06
F, R, W, C, LAT, H, CLIPS = 4, 2, 160, 384, 16, 32, 8
POS = F * R * W
LANES = 256
MESH = pl.DeviceIdType.MESH
BF, F32 = jnp.bfloat16, jnp.float32

WAVES = (
    ((1, 7), ((9, 2), (63, 8)), "zy"),
    ((4,), ((40, 5),), "yz"),
    ((0, 8), ((0, 9),), "zy"),
    ((2, 6), ((20, 7), (60, 3)), "xy"),
    ((3, 5), ((27, 4), (45, 6)), "yz"),
)
OWN = 44
FIXED = 80
PAIRS = sum((n + 1) // 2 for _, ranges, _ in WAVES for _, n in ranges)

SCHEDULE = (
    ("G", 1), ("G", 7), (0, 0), ("G", 4), (1, 0), ("T", "late1"), ("G", 5), ("G", 3), (4, 0), (0, 1),
    ("T", "late0"), (1, 1), ("G", 6), ("G", 2), (3, 0), ("G", 0), (4, 1), ("A", 3), ("G", 8), (2, 0), (3, 1),
    ("A", 8), (1, 2), ("A", 6), (2, 1), ("A", 5), (0, 2), ("T", "hidden"), (1, 3), (4, 2), (1, 4), (3, 2),
    (0, 3), ("T", "clip"), (2, 2), (0, 4), (4, 3), (3, 3), (2, 3), (4, 4), ("T", "out"), (2, 4), (3, 4),
)


def dot(a, b, ca, cb):
    return lax.dot_general(a, b, (((ca,), (cb,)), ((), ())), preferred_element_type=F32)


def sigmoid(v):
    return 1.0 / (1.0 + jnp.exp(-v))


def roll(v, shift):
    return pltpu.roll(v, shift % 128, 1) if shift % 128 else v


def pack(tiles, ref):
    rest, dtype = None, ref.dtype
    for f in range(F):
        ref[f] = tiles[f][:, :128].astype(dtype)
        part = roll(tiles[f][:, 128:], 32 * f)
        rest = part if rest is None else rest + part
    ref[F] = rest.astype(dtype)


def unpack(ref, slot):
    owner, j = slot // F, slot % F
    rest = ref[owner, F].astype(F32)
    out = rest
    for k in range(1, F):
        out = jnp.where(j == k, roll(rest, -32 * k), out)
    out = jnp.where(lax.broadcasted_iota(jnp.int32, out.shape, 1) < 32, out, 0.0)
    return jnp.concatenate([ref[owner, j].astype(F32), out], axis=1)


def as_column(ref):
    return jnp.broadcast_to(ref[...].reshape(1, C), (8, C)).T[:, :1]


def kernel(
    route, lengths, lat_in, cot_in, ink, bias_in, gain_in, ker_in,
    out_lat, out_wg,
    cotbuf, cot3, kbuf, tr1, tr2, stage, latg, lat4, s3, xt, hid, act, inv_ref, ag, hg, yt, lg, lgs, lgr, latg2,
    gbuf, own, ra, sb, q, fin, fr, outf,
    local_sem, send_sem, recv_sem,
):
    clip, tile = lax.axis_index("clip"), lax.axis_index("tile")
    x, core = clip // 2, clip % 2
    z, y = tile // 4, tile % 4
    me = {"clip": clip, "tile": tile}

    def at(**kw):
        d = {**me, **kw}
        return (d["clip"], d["tile"])

    sib = at(clip=2 * x + 1 - core)
    xp, xm, xo = (at(clip=2 * ((x + k) % 4) + core) for k in (1, 3, 2))
    others = tuple(at(clip=2 * ((x + k) % 4) + 1 - core) for k in (1, 3, 2))
    group = (xp, xm, xo) + others + (sib,)
    zp, zm, zo = (at(tile=4 * ((z + k) % 4) + y) for k in (1, 3, 2))
    yp, ym, yo = (at(tile=4 * z + (y + k) % 4) for k in (1, 3, 2))
    tp, tm = (at(tile=(tile + k) % 16) for k in (1, 15))
    peers = (sib, xp, xm, xo, zp, zm, zo, yp, ym, yo, tp, tm) + others

    copies = []

    def send(src, dst, device):
        n = len(copies)
        assert n < FIXED
        cp = pltpu.make_async_remote_copy(
            src_ref=src, dst_ref=dst, send_sem=send_sem.at[n], recv_sem=recv_sem.at[n],
            device_id=device, device_id_type=MESH,
        )
        copies.append(cp)
        cp.start()
        return cp

    load_cot = pltpu.make_async_copy(cot_in.at[0], cotbuf.at[:, 1:3], local_sem.at[0])
    load_cot.start()
    load_ker = pltpu.make_async_copy(ker_in, kbuf, local_sem.at[1])
    load_ker.start()

    barrier = pltpu.get_barrier_semaphore()
    for p in peers:
        pl.semaphore_signal(barrier, inc=1, device_id=p, device_id_type=MESH)
    def greet(p):
        pl.semaphore_signal(barrier, inc=1, device_id=p, device_id_type=MESH)

    for k in (1, 2, 3):
        greet(at(clip=2 * z + core, tile=4 * ((z + k) % 4) + y))
    pl.when(x != z)(lambda: greet(at(clip=2 * z + core, tile=4 * z + y)))

    lane16 = lax.broadcasted_iota(jnp.int32, (20, 128), 1) // LAT
    flat = jnp.concatenate([lat_in[j].astype(F32) for j in range(F)], axis=0)
    for g in range(20):
        tr1[pl.ds(g, 8, stride=24), :] = flat[:, 128 * g : 128 * (g + 1)]
    tr2[W:] = jnp.zeros((LANES - W, 128), F32)
    for q8 in range(8):
        u = jnp.zeros((20, 128), F32)
        for jr in range(8):
            u = jnp.where(lane16 == jr, roll(tr1[jr * 24 : jr * 24 + 20], LAT * (jr - q8)), u)
        tr2[pl.ds(q8, 20, stride=8), :] = u
    pack(tr2[...].T.reshape(F, R * LAT, LANES), stage)

    pl.semaphore_wait(barrier, len(peers) + 3 + jnp.where(x != z, 1, 0))

    lat_g = [send(stage, latg.at[clip], d) for d in group]
    parts = (slice(2, 4), slice(1, 2), slice(0, 1))
    halo = [
        [
            send(cot_in.at[0, part, 0], cotbuf.at[part, 3], tm),
            send(cot_in.at[0, part, 1], cotbuf.at[part, 0], tp),
        ]
        for part in parts
    ]
    latg[clip] = stage[...]

    length = lengths[clip]
    live = [jnp.where(f < length, 1.0, 0.0).astype(F32) for f in range(F)]
    top = jnp.where(tile > 0, 1.0, 0.0).astype(F32)
    bottom = jnp.where(tile < 15, 1.0, 0.0).astype(F32)
    edge = (top, 1.0, 1.0, bottom)

    def build_cot(rows, frames):
        col = lax.broadcasted_iota(jnp.int32, (W, C), 0)
        for f in frames:
            for r in rows:
                v = cotbuf[f, r].astype(F32) * (live[f] * edge[r])
                after = jnp.where(col == W - 1, 0.0, pltpu.roll(v, W - 1, 0))
                before = jnp.where(col == 0, 0.0, pltpu.roll(v, 1, 0))
                cot3[f, r, :, 0:C] = after.astype(BF)
                cot3[f, r, :, C : 2 * C] = v.astype(BF)
                cot3[f, r, :, 2 * C : 3 * C] = before.astype(BF)

    def window(dt, dy):
        return cot3[2 - dt : 4, 2 - dy : 4 - dy].reshape((dt + 2) * R * W, 3 * C)

    def act_grad_part(dt, dy, first):
        t0 = 9 * dt + 3 * dy
        taps = jnp.concatenate([kbuf[(t0 + d) * C : (t0 + d + 1) * C] for d in range(3)], axis=1)
        out = dot(taps, window(dt, dy), 1, 1)
        n = (dt + 2) * R * W
        if first:
            ag[...] = out
        else:
            ag[:, :n] += out

    def late_rows(k):
        for cp in halo[k]:
            cp.wait_recv()
        build_cot((0, 3), range(F)[parts[k]])

    load_cot.wait()
    build_cot((1, 2), range(F))

    load_ker.wait()
    act_grad_part(2, 1, True)
    act_grad_part(1, 1, False)
    act_grad_part(0, 1, False)
    for cp in lat_g:
        cp.wait_recv()

    for f in range(F):
        slot = jnp.int32(0)
        for s in range(CLIPS * F):
            slot = jnp.where(route[s] == clip * F + f, s, slot)
        v = unpack(latg, slot) * live[f]
        lat4[f, 1] = v[:LAT].astype(BF)
        lat4[f, 2] = v[LAT:].astype(BF)
    lat_h = [send(lat4.at[:, 1], lat4.at[:, 3], tm), send(lat4.at[:, 2], lat4.at[:, 0], tp)]
    late_rows(0)
    act_grad_part(0, 0, False)
    act_grad_part(0, 2, False)
    for cp in lat_h:
        cp.wait_recv()

    for f in range(F):
        for r in range(4):
            v = lat4[f, r].astype(F32) * edge[r]
            s3[f, r, 0:LAT] = pltpu.roll(v, 1, 1).astype(BF)
            s3[f, r, LAT : 2 * LAT] = v.astype(BF)
            s3[f, r, 2 * LAT :] = pltpu.roll(v, LANES - 1, 1).astype(BF)
    for f in range(F):
        for r in range(R):
            for dt in range(3):
                for dy in range(3):
                    at_rows = slice((3 * dt + dy) * 48, (3 * dt + dy + 1) * 48)
                    at_cols = slice((2 * f + r) * W, (2 * f + r + 1) * W)
                    if f - 2 + dt >= 0:
                        xt[at_rows, at_cols] = s3[f - 2 + dt, r + dy, :, 0:W]
                    else:
                        xt[at_rows, at_cols] = jnp.zeros((48, W), BF)
    gain = as_column(gain_in)
    hid[...] = dot(ink[...], xt[...], 0, 0) + as_column(bias_in)

    def norm_step(n, carry):
        cols = pl.ds(pl.multiple_of(n * 128, 128), 128)
        h = hid[:, cols]
        inv = lax.rsqrt(jnp.mean(h * h, axis=0, keepdims=True) + EPS)
        normed = h * inv * gain
        act[:, cols] = (normed * sigmoid(normed)).astype(BF)
        inv_ref[:, cols] = inv
        return carry

    lax.fori_loop(0, POS // 128, norm_step, 0)

    def weight_part(g, order):
        dt, dy = g // 3, g % 3
        out = dot(act[:, : (dt + 2) * R * W], window(dt, dy), 1, 0)
        for k in range(9):
            v = out[:, 128 * k : 128 * (k + 1)]
            if order == "yz":
                v = jnp.concatenate(
                    [v[24 * (4 * b + a) : 24 * (4 * b + a) + 24] for a in range(4) for b in range(4)], axis=0
                )
            gbuf[9 * g + k] = v.astype(BF)

    def pick(a, b):
        return jnp.where(core == 0, a, b)

    to_owner = []

    def wave_steps(ranges, order, off, poff):
        total = sum(n for _, n in ranges)
        mine = pl.ds(off, total)
        if order == "zy":
            (a, ap, am, ao), (b, bp, bm, bo) = (z, zp, zm, zo), (y, yp, ym, yo)
        elif order == "yz":
            (a, ap, am, ao), (b, bp, bm, bo) = (y, yp, ym, yo), (z, zp, zm, zo)
        else:
            (a, ap, am, ao), (b, bp, bm, bo) = (x, xp, xm, xo), (y, yp, ym, yo)
        st = {}

        def rows_a(k):
            return pl.ds(pl.multiple_of(96 * ((a + k) % 4), 96), 96)

        def s0():
            st["c"], at0 = [], off
            for first, n in ranges:
                mirror = 81 - first - n
                src = gbuf.at[pl.ds(pick(mirror, first), n)]
                st["c"].append(send(src, own.at[pl.ds(at0, n)], sib))
                at0 += n

        def s1():
            for cp in st["c"]:
                cp.wait_recv()
            at0 = off
            for first, n in ranges:
                start = pick(first, 81 - first - n)

                def body(k, carry, start=start, at0=at0):
                    own[at0 + k] = own[at0 + k] + gbuf[start + k]
                    return carry

                lax.fori_loop(0, n, body, 0, unroll=True)
                at0 += n
            st["a"] = [
                send(own.at[mine, rows_a(k)], ra.at[mine, i], device)
                for i, (k, device) in enumerate(((1, ap), (3, am), (2, ao)))
            ]

        def s2():
            for cp in st["a"]:
                cp.wait_recv()
            rows = rows_a(0)

            def block(i):
                v = own[i, rows].astype(F32) + ra[i, 0].astype(F32)
                return v + ra[i, 1].astype(F32) + ra[i, 2].astype(F32)

            at0, p = off, poff
            for _, n in ranges:
                for i in range(at0, at0 + n, 2):
                    one = block(i)
                    two = block(i + 1) if i + 1 < at0 + n else jnp.zeros_like(one)
                    for to in range(4):
                        part = slice(24 * to, 24 * to + 24)
                        sb[to, p] = jnp.concatenate([one[part], two[part]], axis=0).astype(BF)
                    p += 1
                at0 += n
            pairs = pl.ds(poff, p - poff)
            st["q"] = [
                send(sb.at[(b + k) % 4, pairs], q.at[i, pairs], device)
                for i, (k, device) in enumerate(((1, bp), (3, bm), (2, bo)))
            ]

        def s3_():
            for cp in st["q"]:
                cp.wait_recv()
            p, st["owner"] = poff, []
            for first, n in ranges:
                count = (n + 1) // 2
                for i in range(p, p + count):
                    v = sb[b, i].astype(F32) + q[0, i].astype(F32)
                    fin[i] = (v + q[1, i].astype(F32) + q[2, i].astype(F32)).astype(BF)
                mirror = 81 - first - n
                owner = pick(first // 20, (mirror - 10) // 20)
                base = FIXED + 4 * len(to_owner)
                slot, to = (z, 4 * x + y) if order == "xy" else (x, tile)
                cp = pltpu.make_async_remote_copy(
                    src_ref=fin.at[pl.ds(p, count)], dst_ref=fr.at[slot, pl.ds(p, count)],
                    send_sem=send_sem.at[base], recv_sem=recv_sem.at[base + slot],
                    device_id=at(clip=2 * owner + core, tile=to), device_id_type=MESH,
                )
                away = (owner != x) | (to != tile)
                to_owner.append((away, cp))
                st["owner"].append((owner, base, p, n, pick(first % 20, (mirror - 10) % 20)))
                pl.when(away)(cp.start)
                p += count

        def s4():
            for owner, base, p, n, place in st["owner"]:

                @pl.when(owner == x)
                def _(base=base, p=p, n=n, place=place):
                    count = (n + 1) // 2
                    slot = z if order == "xy" else x
                    others = [(slot + k) % 4 for k in (1, 3, 2)]
                    mine = pl.ds(p, count)

                    def arrive(k):
                        pltpu.make_async_remote_copy(
                            src_ref=fin.at[mine], dst_ref=fr.at[k, mine],
                            send_sem=send_sem.at[base], recv_sem=recv_sem.at[base + k],
                            device_id=xp, device_id_type=MESH,
                        ).wait_recv()

                    for k in others:
                        arrive(k)
                    if order == "xy":
                        pl.when(x != z)(lambda: arrive(z))

                        @pl.when(x == z)
                        def _():
                            fr[z, mine] = fin[mine]

                    for i in range(count):
                        v = (fr[z, p + i] if order == "xy" else fin[p + i]).astype(F32)
                        for k in others:
                            v += fr[k, p + i].astype(F32)
                        outf[place + 2 * i] = v[:24]
                        if 2 * i + 1 < n:
                            outf[place + 2 * i + 1] = v[24:]

        return [s0, s1, s2, s3_, s4]

    waves, off, poff = [], 0, 0
    for _, ranges, order in WAVES:
        waves.append(wave_steps(ranges, order, off, poff))
        off += sum(n for _, n in ranges)
        poff += sum((n + 1) // 2 for _, n in ranges)
    orders = {g: order for groups, _, order in WAVES for g in groups}

    def hidden_grad():
        def grad_step(n, carry):
            cols = pl.ds(pl.multiple_of(n * 128, 128), 128)
            h, inv = hid[:, cols], inv_ref[:, cols]
            normed = h * inv * gain
            s = sigmoid(normed)
            gained = ag[:, cols] * s * (1.0 + normed * (1.0 - s)) * gain
            inner = jnp.mean(gained * h, axis=0, keepdims=True)
            hg[:, cols] = (inv * gained - h * (inv * inv * inv * inner)).astype(BF)
            return carry

        lax.fori_loop(0, POS // 128, grad_step, 0)
        yt[...] = dot(ink[...], hg[...], 1, 0)

        col = lax.broadcasted_iota(jnp.int32, (LAT, POS), 1) % W
        summed = []
        for g in range(9):
            base = 48 * g
            after = jnp.where(col == W - 1, 0.0, pltpu.roll(yt[base : base + LAT], POS - 1, 1))
            before = jnp.where(col == 0, 0.0, pltpu.roll(yt[base + 2 * LAT : base + 3 * LAT], 1, 1))
            summed.append(yt[base + LAT : base + 2 * LAT] + after + before)
        for f in range(F):
            for r in range(4):
                total = None
                for dt in range(3):
                    for dy in range(3):
                        fh, rh = f + 2 - dt, r - dy
                        if fh < F and 0 <= rh < R:
                            p = (2 * fh + rh) * W
                            term = summed[3 * dt + dy][:, p : p + W]
                            total = term if total is None else total + term
                lg[f, r, :, 0:W] = total
                lg[f, r, :, W:] = jnp.zeros((LAT, LANES - W), F32)
        pack([lg[f, 0] for f in range(F)], lgs.at[0])
        pack([lg[f, 3] for f in range(F)], lgs.at[1])
        st["lg"] = [send(lgs.at[0], lgr.at[1], tm), send(lgs.at[1], lgr.at[0], tp)]

    def clip_grad():
        for cp in st["lg"]:
            cp.wait_recv()
        tiles = []
        narrow = lax.broadcasted_iota(jnp.int32, (LAT, 128), 1) < 32
        for f in range(F):
            from_up, from_down = (
                jnp.concatenate(
                    [lgr[k, f], jnp.where(narrow, roll(lgr[k, F], -32 * f), 0.0)], axis=1
                )
                for k in range(2)
            )
            first = (lg[f, 1] + from_up * top) * live[f]
            second = (lg[f, 2] + from_down * bottom) * live[f]
            tiles.append(jnp.concatenate([first, second], axis=0))
        pack(tiles, latg2.at[clip])
        st["back"] = [send(latg2.at[clip], latg2.at[clip], d) for d in group]

    def latent_grad():
        for cp in st["back"]:
            cp.wait_recv()
        tiles = [unpack(latg2, route[clip * F + j]) for j in range(F)]
        tr2[...] = jnp.concatenate(tiles, axis=0).T
        for jr in range(8):
            u = jnp.zeros((20, 128), F32)
            for q8 in range(8):
                u = jnp.where(lane16 == q8, roll(tr2[pl.ds(q8, 20, stride=8), :], LAT * (q8 - jr)), u)
            tr1[jr * 24 : jr * 24 + 20] = u
        flat = jnp.concatenate([tr1[pl.ds(g, 8, stride=24), :] for g in range(20)], axis=1)
        for j in range(F):
            out_lat[j] = flat[R * j : R * j + R].astype(BF)

    st = {}
    tail = {"late1": lambda: late_rows(1), "late0": lambda: late_rows(2), "hidden": hidden_grad, "clip": clip_grad, "out": latent_grad}
    for kind, k in SCHEDULE:
        if kind == "G":
            weight_part(k, orders[k])
        elif kind == "A":
            act_grad_part(k // 3, k % 3, False)
        elif kind == "T":
            tail[k]()
        else:
            waves[kind][k]()

    scale = 1.0 / math.sqrt(CLIPS * F * H * W)
    flat = jnp.concatenate([outf[k] * scale for k in range(11)], axis=1)
    out_wg[...] = pltpu.roll(flat, 11 * 128 - 16 * clip, 1)[:, :1296]

    for cp in copies:
        cp.wait_send()
    for away, cp in to_owner:
        pl.when(away)(cp.wait_send)


def on_device(latents, tile_route, lengths, reward_grad, in_kernel, in_bias, norm_gain, kernel_):
    vmem = pl.BlockSpec(memory_space=pltpu.VMEM)
    smem = pl.BlockSpec(memory_space=pltpu.SMEM)
    hbm = pl.BlockSpec(memory_space=pl.ANY)

    def v(*shape, dtype=BF):
        return pltpu.VMEM(shape, dtype)

    return pl.pallas_call(
        kernel,
        out_shape=(
            jax.ShapeDtypeStruct((F, R, W * LAT), BF),
            jax.ShapeDtypeStruct((24, 1296), F32),
        ),
        in_specs=[smem, smem, vmem, hbm, vmem, vmem, vmem, hbm],
        out_specs=(vmem, vmem),
        scratch_shapes=[
            v(F, 4, W, C),
            v(F, 4, W, 3 * C),
            v(27 * C, C),
            v(192, 128, dtype=F32),
            v(LANES, 128, dtype=F32),
            v(F + 1, R * LAT, 128),
            v(CLIPS, F + 1, R * LAT, 128),
            v(F, 4, LAT, LANES),
            v(F, 4, 3 * LAT, LANES),
            v(27 * LAT, POS),
            v(C, POS, dtype=F32),
            v(C, POS),
            v(1, POS, dtype=F32),
            v(C, POS, dtype=F32),
            v(C, POS),
            v(27 * LAT, POS, dtype=F32),
            v(F, 4, LAT, LANES, dtype=F32),
            v(2, F + 1, LAT, 128, dtype=F32),
            v(2, F + 1, LAT, 128, dtype=F32),
            v(CLIPS, F + 1, R * LAT, 128),
            v(81, C, 128),
            v(OWN, C, 128),
            v(OWN, 3, 96, 128),
            v(4, PAIRS, 48, 128),
            v(3, PAIRS, 48, 128),
            v(PAIRS, 48, 128),
            v(4, PAIRS, 48, 128),
            v(11, 24, 128, dtype=F32),
            pltpu.SemaphoreType.DMA((2,)),
            pltpu.SemaphoreType.DMA((FIXED + 36,)),
            pltpu.SemaphoreType.DMA((FIXED + 36,)),
        ],
        compiler_params=pltpu.CompilerParams(
            collective_id=0, has_side_effects=True, vmem_limit_bytes=62 * 2**20
        ),
        name="backward",
    )(
        tile_route, lengths, latents, reward_grad, in_kernel, in_bias, norm_gain, kernel_,
    )


def solution(mesh):
    return jax.shard_map(
        on_device,
        mesh=mesh,
        in_specs=(
            P("clip", "tile", None),
            P(),
            P(),
            P("clip", None, "tile", None, None),
            P(),
            P(),
            P(),
            P(),
        ),
        out_specs=(P("clip", "tile", None), P("tile", "clip")),
        check_vma=False,
    )
```

```python
import math

import jax
import jax.numpy as jnp
from jax import lax
from jax.experimental import pallas as pl
from jax.experimental.pallas import tpu as pltpu
from jax.sharding import PartitionSpec as P

EPS = 1e-06
F, R, W, C, LAT, H, CLIPS = 4, 2, 160, 384, 16, 32, 8
POS = F * R * W
LANES = 256
MESH = pl.DeviceIdType.MESH
BF, F32 = jnp.bfloat16, jnp.float32

WAVES = (
    ((1, 7), ((9, 2), (63, 8)), "zy"),
    ((4,), ((40, 5),), "yz"),
    ((0, 8), ((0, 9),), "yz"),
    ((2, 6), ((20, 7), (60, 3)), "zy"),
    ((3, 5), ((27, 4), (45, 6)), "xy"),
)
OWN = 44
FIXED = 80
PAIRS = sum((n + 1) // 2 for _, ranges, _ in WAVES for _, n in ranges)

SCHEDULE = (
    ("G", 1), ("G", 7), (0, 0), ("T", "late1"), ("T", "late0"), ("G", 8), ("G", 0), (2, 0), ("G", 5), (0, 1),
    ("G", 3), (4, 0), ("G", 2), (2, 1), ("G", 6), (3, 0), ("G", 4), (1, 0), (4, 1), ("A", 6), ("A", 3),
    (3, 1), (1, 1), ("A", 8), ("A", 5), ("T", "hidden"), (0, 2), (2, 2), (4, 2), (1, 2), ("T", "clip"),
    (3, 2), (0, 3), (2, 3), (4, 3), (1, 3), (0, 4), (3, 3), (2, 4), ("T", "out"), (1, 4), (4, 4), (3, 4),
)


def dot(a, b, ca, cb):
    return lax.dot_general(a, b, (((ca,), (cb,)), ((), ())), preferred_element_type=F32)


def sigmoid(v):
    return 1.0 / (1.0 + jnp.exp(-v))


def roll(v, shift):
    return pltpu.roll(v, shift % 128, 1) if shift % 128 else v


def pack(tiles, ref):
    rest, dtype = None, ref.dtype
    for f in range(F):
        ref[f] = tiles[f][:, :128].astype(dtype)
        part = roll(tiles[f][:, 128:], 32 * f)
        rest = part if rest is None else rest + part
    ref[F] = rest.astype(dtype)


def unpack(ref, slot):
    owner, j = slot // F, slot % F
    rest = ref[owner, F].astype(F32)
    out = rest
    for k in range(1, F):
        out = jnp.where(j == k, roll(rest, -32 * k), out)
    out = jnp.where(lax.broadcasted_iota(jnp.int32, out.shape, 1) < 32, out, 0.0)
    return jnp.concatenate([ref[owner, j].astype(F32), out], axis=1)


def as_column(ref):
    return jnp.broadcast_to(ref[...].reshape(1, C), (8, C)).T[:, :1]


def kernel(
    route, lengths, lat_in, cot_in, ink, bias_in, gain_in, ker_in,
    out_lat, out_wg,
    cotbuf, cot3, kbuf, tr1, tr2, stage, latg, lat4, s3, xt, hid, act, inv_ref, ag, hg, yt, lg, lgs, lgr, latg2,
    gbuf, own, ra, sb, q, fin, fr, outf,
    local_sem, send_sem, recv_sem,
):
    clip, tile = lax.axis_index("clip"), lax.axis_index("tile")
    x, core = clip // 2, clip % 2
    z, y = tile // 4, tile % 4
    me = {"clip": clip, "tile": tile}

    def at(**kw):
        d = {**me, **kw}
        return (d["clip"], d["tile"])

    sib = at(clip=2 * x + 1 - core)
    xp, xm, xo = (at(clip=2 * ((x + k) % 4) + core) for k in (1, 3, 2))
    others = tuple(at(clip=2 * ((x + k) % 4) + 1 - core) for k in (1, 3, 2))
    group = (xp, xm, xo) + others + (sib,)
    zp, zm, zo = (at(tile=4 * ((z + k) % 4) + y) for k in (1, 3, 2))
    yp, ym, yo = (at(tile=4 * z + (y + k) % 4) for k in (1, 3, 2))
    tp, tm = (at(tile=(tile + k) % 16) for k in (1, 15))
    peers = (sib, xp, xm, xo, zp, zm, zo, yp, ym, yo, tp, tm) + others

    copies = []

    def send(src, dst, device):
        n = len(copies)
        assert n < FIXED
        cp = pltpu.make_async_remote_copy(
            src_ref=src, dst_ref=dst, send_sem=send_sem.at[n], recv_sem=recv_sem.at[n],
            device_id=device, device_id_type=MESH,
        )
        copies.append(cp)
        cp.start()
        return cp

    load_cot = pltpu.make_async_copy(cot_in.at[0], cotbuf.at[:, 1:3], local_sem.at[0])
    load_cot.start()
    load_ker = pltpu.make_async_copy(ker_in, kbuf, local_sem.at[1])
    load_ker.start()

    barrier = pltpu.get_barrier_semaphore()
    for p in peers:
        pl.semaphore_signal(barrier, inc=1, device_id=p, device_id_type=MESH)
    def greet(p):
        pl.semaphore_signal(barrier, inc=1, device_id=p, device_id_type=MESH)

    for k in (1, 2, 3):
        greet(at(clip=2 * z + core, tile=4 * ((z + k) % 4) + y))
    pl.when(x != z)(lambda: greet(at(clip=2 * z + core, tile=4 * z + y)))

    lane16 = lax.broadcasted_iota(jnp.int32, (20, 128), 1) // LAT
    flat = jnp.concatenate([lat_in[j].astype(F32) for j in range(F)], axis=0)
    for g in range(20):
        tr1[pl.ds(g, 8, stride=24), :] = flat[:, 128 * g : 128 * (g + 1)]
    tr2[W:] = jnp.zeros((LANES - W, 128), F32)
    for q8 in range(8):
        u = jnp.zeros((20, 128), F32)
        for jr in range(8):
            u = jnp.where(lane16 == jr, roll(tr1[jr * 24 : jr * 24 + 20], LAT * (jr - q8)), u)
        tr2[pl.ds(q8, 20, stride=8), :] = u
    pack(tr2[...].T.reshape(F, R * LAT, LANES), stage)

    pl.semaphore_wait(barrier, len(peers) + 3 + jnp.where(x != z, 1, 0))

    lat_g = [send(stage, latg.at[clip], d) for d in group]
    parts = (slice(2, 4), slice(1, 2), slice(0, 1))
    halo = [
        [
            send(cot_in.at[0, part, 0], cotbuf.at[part, 3], tm),
            send(cot_in.at[0, part, 1], cotbuf.at[part, 0], tp),
        ]
        for part in parts
    ]
    latg[clip] = stage[...]

    length = lengths[clip]
    live = [jnp.where(f < length, 1.0, 0.0).astype(F32) for f in range(F)]
    top = jnp.where(tile > 0, 1.0, 0.0).astype(F32)
    bottom = jnp.where(tile < 15, 1.0, 0.0).astype(F32)
    edge = (top, 1.0, 1.0, bottom)

    def build_cot(rows, frames):
        col = lax.broadcasted_iota(jnp.int32, (W, C), 0)
        for f in frames:
            for r in rows:
                v = cotbuf[f, r].astype(F32) * (live[f] * edge[r])
                after = jnp.where(col == W - 1, 0.0, pltpu.roll(v, W - 1, 0))
                before = jnp.where(col == 0, 0.0, pltpu.roll(v, 1, 0))
                cot3[f, r, :, 0:C] = after.astype(BF)
                cot3[f, r, :, C : 2 * C] = v.astype(BF)
                cot3[f, r, :, 2 * C : 3 * C] = before.astype(BF)

    def window(dt, dy):
        return cot3[2 - dt : 4, 2 - dy : 4 - dy].reshape((dt + 2) * R * W, 3 * C)

    def act_grad_part(dt, dy, first):
        t0 = 9 * dt + 3 * dy
        taps = jnp.concatenate([kbuf[(t0 + d) * C : (t0 + d + 1) * C] for d in range(3)], axis=1)
        out = dot(taps, window(dt, dy), 1, 1)
        n = (dt + 2) * R * W
        if first:
            ag[...] = out
        else:
            ag[:, :n] += out

    def late_rows(k):
        for cp in halo[k]:
            cp.wait_recv()
        build_cot((0, 3), range(F)[parts[k]])

    load_cot.wait()
    build_cot((1, 2), range(F))

    load_ker.wait()
    act_grad_part(2, 1, True)
    act_grad_part(1, 1, False)
    act_grad_part(0, 1, False)
    for cp in lat_g:
        cp.wait_recv()

    for f in range(F):
        slot = jnp.int32(0)
        for s in range(CLIPS * F):
            slot = jnp.where(route[s] == clip * F + f, s, slot)
        v = unpack(latg, slot) * live[f]
        lat4[f, 1] = v[:LAT].astype(BF)
        lat4[f, 2] = v[LAT:].astype(BF)
    lat_h = [send(lat4.at[:, 1], lat4.at[:, 3], tm), send(lat4.at[:, 2], lat4.at[:, 0], tp)]
    late_rows(0)
    act_grad_part(0, 0, False)
    act_grad_part(0, 2, False)
    for cp in lat_h:
        cp.wait_recv()

    for f in range(F):
        for r in range(4):
            v = lat4[f, r].astype(F32) * edge[r]
            s3[f, r, 0:LAT] = pltpu.roll(v, 1, 1).astype(BF)
            s3[f, r, LAT : 2 * LAT] = v.astype(BF)
            s3[f, r, 2 * LAT :] = pltpu.roll(v, LANES - 1, 1).astype(BF)
    for f in range(F):
        for r in range(R):
            for dt in range(3):
                for dy in range(3):
                    at_rows = slice((3 * dt + dy) * 48, (3 * dt + dy + 1) * 48)
                    at_cols = slice((2 * f + r) * W, (2 * f + r + 1) * W)
                    if f - 2 + dt >= 0:
                        xt[at_rows, at_cols] = s3[f - 2 + dt, r + dy, :, 0:W]
                    else:
                        xt[at_rows, at_cols] = jnp.zeros((48, W), BF)
    gain = as_column(gain_in)
    hid[...] = dot(ink[...], xt[...], 0, 0) + as_column(bias_in)

    def norm_step(n, carry):
        cols = pl.ds(pl.multiple_of(n * 128, 128), 128)
        h = hid[:, cols]
        inv = lax.rsqrt(jnp.mean(h * h, axis=0, keepdims=True) + EPS)
        normed = h * inv * gain
        act[:, cols] = (normed * sigmoid(normed)).astype(BF)
        inv_ref[:, cols] = inv
        return carry

    lax.fori_loop(0, POS // 128, norm_step, 0)

    def weight_part(g, order):
        dt, dy = g // 3, g % 3
        out = dot(act[:, : (dt + 2) * R * W], window(dt, dy), 1, 0)
        for k in range(9):
            v = out[:, 128 * k : 128 * (k + 1)]
            if order == "yz":
                v = jnp.concatenate(
                    [v[24 * (4 * b + a) : 24 * (4 * b + a) + 24] for a in range(4) for b in range(4)], axis=0
                )
            gbuf[9 * g + k] = v.astype(BF)

    def pick(a, b):
        return jnp.where(core == 0, a, b)

    to_owner = []

    def wave_steps(ranges, order, off, poff):
        total = sum(n for _, n in ranges)
        mine = pl.ds(off, total)
        if order == "zy":
            (a, ap, am, ao), (b, bp, bm, bo) = (z, zp, zm, zo), (y, yp, ym, yo)
        elif order == "yz":
            (a, ap, am, ao), (b, bp, bm, bo) = (y, yp, ym, yo), (z, zp, zm, zo)
        else:
            (a, ap, am, ao), (b, bp, bm, bo) = (x, xp, xm, xo), (y, yp, ym, yo)
        st = {}

        def rows_a(k):
            return pl.ds(pl.multiple_of(96 * ((a + k) % 4), 96), 96)

        def s0():
            st["c"], at0 = [], off
            for first, n in ranges:
                mirror = 81 - first - n
                src = gbuf.at[pl.ds(pick(mirror, first), n)]
                st["c"].append(send(src, own.at[pl.ds(at0, n)], sib))
                at0 += n

        def s1():
            for cp in st["c"]:
                cp.wait_recv()
            at0 = off
            for first, n in ranges:
                start = pick(first, 81 - first - n)

                def body(k, carry, start=start, at0=at0):
                    own[at0 + k] = own[at0 + k] + gbuf[start + k]
                    return carry

                lax.fori_loop(0, n, body, 0, unroll=True)
                at0 += n
            st["a"] = [
                send(own.at[mine, rows_a(k)], ra.at[mine, i], device)
                for i, (k, device) in enumerate(((1, ap), (3, am), (2, ao)))
            ]

        def s2():
            for cp in st["a"]:
                cp.wait_recv()
            rows = rows_a(0)

            def block(i):
                v = own[i, rows].astype(F32) + ra[i, 0].astype(F32)
                return v + ra[i, 1].astype(F32) + ra[i, 2].astype(F32)

            at0, p = off, poff
            for _, n in ranges:
                for i in range(at0, at0 + n, 2):
                    one = block(i)
                    two = block(i + 1) if i + 1 < at0 + n else jnp.zeros_like(one)
                    for to in range(4):
                        part = slice(24 * to, 24 * to + 24)
                        sb[to, p] = jnp.concatenate([one[part], two[part]], axis=0).astype(BF)
                    p += 1
                at0 += n
            pairs = pl.ds(poff, p - poff)
            st["q"] = [
                send(sb.at[(b + k) % 4, pairs], q.at[i, pairs], device)
                for i, (k, device) in enumerate(((1, bp), (3, bm), (2, bo)))
            ]

        def s3_():
            for cp in st["q"]:
                cp.wait_recv()
            p, st["owner"] = poff, []
            for first, n in ranges:
                count = (n + 1) // 2
                for i in range(p, p + count):
                    v = sb[b, i].astype(F32) + q[0, i].astype(F32)
                    fin[i] = (v + q[1, i].astype(F32) + q[2, i].astype(F32)).astype(BF)
                mirror = 81 - first - n
                owner = pick(first // 20, (mirror - 10) // 20)
                base = FIXED + 4 * len(to_owner)
                slot, to = (z, 4 * x + y) if order == "xy" else (x, tile)
                cp = pltpu.make_async_remote_copy(
                    src_ref=fin.at[pl.ds(p, count)], dst_ref=fr.at[slot, pl.ds(p, count)],
                    send_sem=send_sem.at[base], recv_sem=recv_sem.at[base + slot],
                    device_id=at(clip=2 * owner + core, tile=to), device_id_type=MESH,
                )
                away = (owner != x) | (to != tile)
                to_owner.append((away, cp))
                st["owner"].append((owner, base, p, n, pick(first % 20, (mirror - 10) % 20)))
                pl.when(away)(cp.start)
                p += count

        def s4():
            for owner, base, p, n, place in st["owner"]:

                @pl.when(owner == x)
                def _(base=base, p=p, n=n, place=place):
                    count = (n + 1) // 2
                    slot = z if order == "xy" else x
                    others = [(slot + k) % 4 for k in (1, 3, 2)]
                    mine = pl.ds(p, count)

                    def arrive(k):
                        pltpu.make_async_remote_copy(
                            src_ref=fin.at[mine], dst_ref=fr.at[k, mine],
                            send_sem=send_sem.at[base], recv_sem=recv_sem.at[base + k],
                            device_id=xp, device_id_type=MESH,
                        ).wait_recv()

                    for k in others:
                        arrive(k)
                    if order == "xy":
                        pl.when(x != z)(lambda: arrive(z))

                        @pl.when(x == z)
                        def _():
                            fr[z, mine] = fin[mine]

                    for i in range(count):
                        v = (fr[z, p + i] if order == "xy" else fin[p + i]).astype(F32)
                        for k in others:
                            v += fr[k, p + i].astype(F32)
                        outf[place + 2 * i] = v[:24]
                        if 2 * i + 1 < n:
                            outf[place + 2 * i + 1] = v[24:]

        return [s0, s1, s2, s3_, s4]

    waves, off, poff = [], 0, 0
    for _, ranges, order in WAVES:
        waves.append(wave_steps(ranges, order, off, poff))
        off += sum(n for _, n in ranges)
        poff += sum((n + 1) // 2 for _, n in ranges)
    orders = {g: order for groups, _, order in WAVES for g in groups}

    def hidden_grad():
        def grad_step(n, carry):
            cols = pl.ds(pl.multiple_of(n * 128, 128), 128)
            h, inv = hid[:, cols], inv_ref[:, cols]
            normed = h * inv * gain
            s = sigmoid(normed)
            gained = ag[:, cols] * s * (1.0 + normed * (1.0 - s)) * gain
            inner = jnp.mean(gained * h, axis=0, keepdims=True)
            hg[:, cols] = (inv * gained - h * (inv * inv * inv * inner)).astype(BF)
            return carry

        lax.fori_loop(0, POS // 128, grad_step, 0)
        yt[...] = dot(ink[...], hg[...], 1, 0)

        col = lax.broadcasted_iota(jnp.int32, (LAT, POS), 1) % W
        summed = []
        for g in range(9):
            base = 48 * g
            after = jnp.where(col == W - 1, 0.0, pltpu.roll(yt[base : base + LAT], POS - 1, 1))
            before = jnp.where(col == 0, 0.0, pltpu.roll(yt[base + 2 * LAT : base + 3 * LAT], 1, 1))
            summed.append(yt[base + LAT : base + 2 * LAT] + after + before)
        for f in range(F):
            for r in range(4):
                total = None
                for dt in range(3):
                    for dy in range(3):
                        fh, rh = f + 2 - dt, r - dy
                        if fh < F and 0 <= rh < R:
                            p = (2 * fh + rh) * W
                            term = summed[3 * dt + dy][:, p : p + W]
                            total = term if total is None else total + term
                lg[f, r, :, 0:W] = total
                lg[f, r, :, W:] = jnp.zeros((LAT, LANES - W), F32)
        pack([lg[f, 0] for f in range(F)], lgs.at[0])
        pack([lg[f, 3] for f in range(F)], lgs.at[1])
        st["lg"] = [send(lgs.at[0], lgr.at[1], tm), send(lgs.at[1], lgr.at[0], tp)]

    def clip_grad():
        for cp in st["lg"]:
            cp.wait_recv()
        tiles = []
        narrow = lax.broadcasted_iota(jnp.int32, (LAT, 128), 1) < 32
        for f in range(F):
            from_up, from_down = (
                jnp.concatenate(
                    [lgr[k, f], jnp.where(narrow, roll(lgr[k, F], -32 * f), 0.0)], axis=1
                )
                for k in range(2)
            )
            first = (lg[f, 1] + from_up * top) * live[f]
            second = (lg[f, 2] + from_down * bottom) * live[f]
            tiles.append(jnp.concatenate([first, second], axis=0))
        pack(tiles, latg2.at[clip])
        st["back"] = [send(latg2.at[clip], latg2.at[clip], d) for d in group]

    def latent_grad():
        for cp in st["back"]:
            cp.wait_recv()
        tiles = [unpack(latg2, route[clip * F + j]) for j in range(F)]
        tr2[...] = jnp.concatenate(tiles, axis=0).T
        for jr in range(8):
            u = jnp.zeros((20, 128), F32)
            for q8 in range(8):
                u = jnp.where(lane16 == q8, roll(tr2[pl.ds(q8, 20, stride=8), :], LAT * (q8 - jr)), u)
            tr1[jr * 24 : jr * 24 + 20] = u
        flat = jnp.concatenate([tr1[pl.ds(g, 8, stride=24), :] for g in range(20)], axis=1)
        for j in range(F):
            out_lat[j] = flat[R * j : R * j + R].astype(BF)

    st = {}
    tail = {"late1": lambda: late_rows(1), "late0": lambda: late_rows(2), "hidden": hidden_grad, "clip": clip_grad, "out": latent_grad}
    for kind, k in SCHEDULE:
        if kind == "G":
            weight_part(k, orders[k])
        elif kind == "A":
            act_grad_part(k // 3, k % 3, False)
        elif kind == "T":
            tail[k]()
        else:
            waves[kind][k]()

    scale = 1.0 / math.sqrt(CLIPS * F * H * W)
    flat = jnp.concatenate([outf[k] * scale for k in range(11)], axis=1)
    out_wg[...] = pltpu.roll(flat, 11 * 128 - 16 * clip, 1)[:, :1296]

    for cp in copies:
        cp.wait_send()
    for away, cp in to_owner:
        pl.when(away)(cp.wait_send)


def hand_out(lat_in, wg_in, lat_out, wg_out):
    lat_out[...] = lat_in[...]
    wg_out[...] = wg_in[...]


def on_device(latents, tile_route, lengths, reward_grad, in_kernel, in_bias, norm_gain, kernel_):
    vmem = pl.BlockSpec(memory_space=pltpu.VMEM)
    smem = pl.BlockSpec(memory_space=pltpu.SMEM)
    hbm = pl.BlockSpec(memory_space=pl.ANY)

    def v(*shape, dtype=BF):
        return pltpu.VMEM(shape, dtype)

    lat_grad, weight_grad = pl.pallas_call(
        kernel,
        out_shape=(
            jax.ShapeDtypeStruct((F, R, W * LAT), BF),
            jax.ShapeDtypeStruct((24, 1296), F32),
        ),
        in_specs=[smem, smem, vmem, hbm, vmem, vmem, vmem, hbm],
        out_specs=(vmem, vmem),
        scratch_shapes=[
            v(F, 4, W, C),
            v(F, 4, W, 3 * C),
            v(27 * C, C),
            v(192, 128, dtype=F32),
            v(LANES, 128, dtype=F32),
            v(F + 1, R * LAT, 128),
            v(CLIPS, F + 1, R * LAT, 128),
            v(F, 4, LAT, LANES),
            v(F, 4, 3 * LAT, LANES),
            v(27 * LAT, POS),
            v(C, POS, dtype=F32),
            v(C, POS),
            v(1, POS, dtype=F32),
            v(C, POS, dtype=F32),
            v(C, POS),
            v(27 * LAT, POS, dtype=F32),
            v(F, 4, LAT, LANES, dtype=F32),
            v(2, F + 1, LAT, 128, dtype=F32),
            v(2, F + 1, LAT, 128, dtype=F32),
            v(CLIPS, F + 1, R * LAT, 128),
            v(81, C, 128),
            v(OWN, C, 128),
            v(OWN, 3, 96, 128),
            v(4, PAIRS, 48, 128),
            v(3, PAIRS, 48, 128),
            v(PAIRS, 48, 128),
            v(4, PAIRS, 48, 128),
            v(11, 24, 128, dtype=F32),
            pltpu.SemaphoreType.DMA((2,)),
            pltpu.SemaphoreType.DMA((FIXED + 36,)),
            pltpu.SemaphoreType.DMA((FIXED + 36,)),
        ],
        compiler_params=pltpu.CompilerParams(
            collective_id=0, has_side_effects=True, vmem_limit_bytes=62 * 2**20
        ),
        name="backward",
    )(
        tile_route, lengths, latents, reward_grad, in_kernel, in_bias, norm_gain, kernel_,
    )
    return pl.pallas_call(
        hand_out,
        out_shape=(
            jax.ShapeDtypeStruct(lat_grad.shape, BF),
            jax.ShapeDtypeStruct(weight_grad.shape, F32),
        ),
        in_specs=[vmem, vmem],
        out_specs=(vmem, vmem),
        name="hand_out",
    )(lat_grad, weight_grad)


def solution(mesh):
    return jax.shard_map(
        on_device,
        mesh=mesh,
        in_specs=(
            P("clip", "tile", None),
            P(),
            P(),
            P("clip", None, "tile", None, None),
            P(),
            P(),
            P(),
            P(),
        ),
        out_specs=(P("clip", "tile", None), P("tile", "clip")),
        check_vma=False,
    )
```

```python
import math

import jax
import jax.numpy as jnp
from jax import lax
from jax.experimental import pallas as pl
from jax.experimental.pallas import tpu as pltpu
from jax.sharding import PartitionSpec as P

EPS = 1e-06
F, R, W, C, LAT, H, CLIPS = 4, 2, 160, 384, 16, 32, 8
POS = F * R * W
LANES = 256
MESH = pl.DeviceIdType.MESH
BF, F32 = jnp.bfloat16, jnp.float32

WAVES = (
    ((1, 7), ((9, 2), (63, 8)), "zy"),
    ((4,), ((40, 5),), "yz"),
    ((0, 8), ((0, 9),), "yz"),
    ((2, 6), ((20, 7), (60, 3)), "zy"),
    ((3, 5), ((27, 4), (45, 6)), "xy"),
)
OWN = 44
FIXED = 80
PAIRS = sum((n + 1) // 2 for _, ranges, _ in WAVES for _, n in ranges)

SCHEDULE = (
    ("G", 1), ("G", 7), (0, 0), ("T", "late1"), ("T", "late0"), ("G", 8), ("G", 0), (2, 0), ("G", 5), (0, 1),
    ("G", 3), (4, 0), ("G", 2), (2, 1), ("G", 6), (3, 0), ("G", 4), (1, 0), (4, 1), ("A", 6), ("A", 3),
    (3, 1), (1, 1), ("A", 8), ("A", 5), ("T", "hidden"), (0, 2), (2, 2), (4, 2), (1, 2), ("T", "clip"),
    (3, 2), (0, 3), (2, 3), (4, 3), (1, 3), (0, 4), (3, 3), (2, 4), ("T", "out"), (1, 4), (4, 4), (3, 4),
)


def dot(a, b, ca, cb):
    return lax.dot_general(a, b, (((ca,), (cb,)), ((), ())), preferred_element_type=F32)


def sigmoid(v):
    return 1.0 / (1.0 + jnp.exp(-v))


def roll(v, shift):
    return pltpu.roll(v, shift % 128, 1) if shift % 128 else v


def pack(tiles, ref):
    rest, dtype = None, ref.dtype
    for f in range(F):
        ref[f] = tiles[f][:, :128].astype(dtype)
        part = roll(tiles[f][:, 128:], 32 * f)
        rest = part if rest is None else rest + part
    ref[F] = rest.astype(dtype)


def unpack(ref, slot):
    owner, j = slot // F, slot % F
    rest = ref[owner, F].astype(F32)
    out = rest
    for k in range(1, F):
        out = jnp.where(j == k, roll(rest, -32 * k), out)
    out = jnp.where(lax.broadcasted_iota(jnp.int32, out.shape, 1) < 32, out, 0.0)
    return jnp.concatenate([ref[owner, j].astype(F32), out], axis=1)


def as_column(ref):
    return jnp.broadcast_to(ref[...].reshape(1, C), (8, C)).T[:, :1]


def kernel(
    route, lengths, lat_in, cot_in, ink, bias_in, gain_in, ker_in,
    out_lat, out_wg,
    cotbuf, cot3, kbuf, tr1, tr2, stage, latg, lat4, s3, xt, hid, act, inv_ref, ag, yt, lg, lgs, lgr, latg2,
    gbuf, own, ra, sb, q, fin, fr, outf,
    local_sem, send_sem, recv_sem,
):
    clip, tile = lax.axis_index("clip"), lax.axis_index("tile")
    x, core = clip // 2, clip % 2
    z, y = tile // 4, tile % 4
    me = {"clip": clip, "tile": tile}

    def at(**kw):
        d = {**me, **kw}
        return (d["clip"], d["tile"])

    sib = at(clip=2 * x + 1 - core)
    xp, xm, xo = (at(clip=2 * ((x + k) % 4) + core) for k in (1, 3, 2))
    others = tuple(at(clip=2 * ((x + k) % 4) + 1 - core) for k in (1, 3, 2))
    group = (xp, xm, xo) + others + (sib,)
    zp, zm, zo = (at(tile=4 * ((z + k) % 4) + y) for k in (1, 3, 2))
    yp, ym, yo = (at(tile=4 * z + (y + k) % 4) for k in (1, 3, 2))
    tp, tm = (at(tile=(tile + k) % 16) for k in (1, 15))
    peers = (sib, xp, xm, xo, zp, zm, zo, yp, ym, yo, tp, tm) + others

    copies = []

    def send(src, dst, device):
        n = len(copies)
        assert n < FIXED
        cp = pltpu.make_async_remote_copy(
            src_ref=src, dst_ref=dst, send_sem=send_sem.at[n], recv_sem=recv_sem.at[n],
            device_id=device, device_id_type=MESH,
        )
        copies.append(cp)
        cp.start()
        return cp

    load_cot = pltpu.make_async_copy(cot_in.at[0], cotbuf.at[:, 1:3], local_sem.at[0])
    load_cot.start()
    load_ker = pltpu.make_async_copy(ker_in, kbuf, local_sem.at[1])
    load_ker.start()

    barrier = pltpu.get_barrier_semaphore()
    for p in peers:
        pl.semaphore_signal(barrier, inc=1, device_id=p, device_id_type=MESH)
    def greet(p):
        pl.semaphore_signal(barrier, inc=1, device_id=p, device_id_type=MESH)

    for k in (1, 2, 3):
        greet(at(clip=2 * z + core, tile=4 * ((z + k) % 4) + y))
    pl.when(x != z)(lambda: greet(at(clip=2 * z + core, tile=4 * z + y)))

    lane16 = lax.broadcasted_iota(jnp.int32, (20, 128), 1) // LAT
    flat = jnp.concatenate([lat_in[j].astype(F32) for j in range(F)], axis=0)
    for g in range(20):
        tr1[pl.ds(g, 8, stride=24), :] = flat[:, 128 * g : 128 * (g + 1)]
    tr2[W:] = jnp.zeros((LANES - W, 128), F32)
    for q8 in range(8):
        u = jnp.zeros((20, 128), F32)
        for jr in range(8):
            u = jnp.where(lane16 == jr, roll(tr1[jr * 24 : jr * 24 + 20], LAT * (jr - q8)), u)
        tr2[pl.ds(q8, 20, stride=8), :] = u
    pack(tr2[...].T.reshape(F, R * LAT, LANES), stage)

    pl.semaphore_wait(barrier, len(peers) + 3 + jnp.where(x != z, 1, 0))

    lat_g = [send(stage, latg.at[clip], d) for d in group]
    parts = (slice(2, 4), slice(1, 2), slice(0, 1))
    halo = [
        [
            send(cot_in.at[0, part, 0], cotbuf.at[part, 3], tm),
            send(cot_in.at[0, part, 1], cotbuf.at[part, 0], tp),
        ]
        for part in parts
    ]
    latg[clip] = stage[...]

    length = lengths[clip]
    live = [jnp.where(f < length, 1.0, 0.0).astype(F32) for f in range(F)]
    top = jnp.where(tile > 0, 1.0, 0.0).astype(F32)
    bottom = jnp.where(tile < 15, 1.0, 0.0).astype(F32)
    edge = (top, 1.0, 1.0, bottom)

    def build_cot(rows, frames):
        col = lax.broadcasted_iota(jnp.int32, (W, C), 0)
        for f in frames:
            for r in rows:
                v = cotbuf[f, r].astype(F32) * (live[f] * edge[r])
                after = jnp.where(col == W - 1, 0.0, pltpu.roll(v, W - 1, 0))
                before = jnp.where(col == 0, 0.0, pltpu.roll(v, 1, 0))
                cot3[f, r, :, 0:C] = after.astype(BF)
                cot3[f, r, :, C : 2 * C] = v.astype(BF)
                cot3[f, r, :, 2 * C : 3 * C] = before.astype(BF)

    def window(dt, dy):
        return cot3[2 - dt : 4, 2 - dy : 4 - dy].reshape((dt + 2) * R * W, 3 * C)

    def act_grad_part(dt, dy, first):
        t0 = 9 * dt + 3 * dy
        taps = jnp.concatenate([kbuf[(t0 + d) * C : (t0 + d + 1) * C] for d in range(3)], axis=1)
        out = dot(taps, window(dt, dy), 1, 1)
        n = (dt + 2) * R * W
        if first:
            ag[...] = out
        else:
            ag[:, :n] += out

    def late_rows(k):
        for cp in halo[k]:
            cp.wait_recv()
        build_cot((0, 3), range(F)[parts[k]])

    load_cot.wait()
    build_cot((1, 2), range(F))

    load_ker.wait()
    act_grad_part(2, 1, True)
    act_grad_part(1, 1, False)
    act_grad_part(0, 1, False)
    for cp in lat_g:
        cp.wait_recv()

    for f in range(F):
        slot = jnp.int32(0)
        for s in range(CLIPS * F):
            slot = jnp.where(route[s] == clip * F + f, s, slot)
        v = unpack(latg, slot) * live[f]
        lat4[f, 1] = v[:LAT].astype(BF)
        lat4[f, 2] = v[LAT:].astype(BF)
    lat_h = [send(lat4.at[:, 1], lat4.at[:, 3], tm), send(lat4.at[:, 2], lat4.at[:, 0], tp)]
    late_rows(0)
    act_grad_part(0, 0, False)
    act_grad_part(0, 2, False)
    for cp in lat_h:
        cp.wait_recv()

    for f in range(F):
        for r in range(4):
            v = lat4[f, r].astype(F32) * edge[r]
            s3[f, r, 0:LAT] = pltpu.roll(v, 1, 1).astype(BF)
            s3[f, r, LAT : 2 * LAT] = v.astype(BF)
            s3[f, r, 2 * LAT :] = pltpu.roll(v, LANES - 1, 1).astype(BF)
    for f in range(F):
        for r in range(R):
            for dt in range(3):
                for dy in range(3):
                    at_rows = slice((3 * dt + dy) * 48, (3 * dt + dy + 1) * 48)
                    at_cols = slice((2 * f + r) * W, (2 * f + r + 1) * W)
                    if f - 2 + dt >= 0:
                        xt[at_rows, at_cols] = s3[f - 2 + dt, r + dy, :, 0:W]
                    else:
                        xt[at_rows, at_cols] = jnp.zeros((48, W), BF)
    gain = as_column(gain_in)
    bias = as_column(bias_in)
    for n in range(0, POS, 256):
        cols = slice(n, n + 256)
        h = dot(ink[...], xt[:, cols], 0, 0) + bias
        hid[:, cols] = h
        inv = lax.rsqrt(jnp.mean(h * h, axis=0, keepdims=True) + EPS)
        normed = h * inv * gain
        act[:, cols] = (normed * sigmoid(normed)).astype(BF)
        inv_ref[:, cols] = inv

    def weight_part(g, order):
        dt, dy = g // 3, g % 3
        out = dot(act[:, : (dt + 2) * R * W], window(dt, dy), 1, 0)
        for k in range(9):
            v = out[:, 128 * k : 128 * (k + 1)]
            if order == "yz":
                v = jnp.concatenate(
                    [v[24 * (4 * b + a) : 24 * (4 * b + a) + 24] for a in range(4) for b in range(4)], axis=0
                )
            gbuf[9 * g + k] = v.astype(BF)

    def pick(a, b):
        return jnp.where(core == 0, a, b)

    to_owner = []

    def wave_steps(ranges, order, off, poff):
        total = sum(n for _, n in ranges)
        mine = pl.ds(off, total)
        if order == "zy":
            (a, ap, am, ao), (b, bp, bm, bo) = (z, zp, zm, zo), (y, yp, ym, yo)
        elif order == "yz":
            (a, ap, am, ao), (b, bp, bm, bo) = (y, yp, ym, yo), (z, zp, zm, zo)
        else:
            (a, ap, am, ao), (b, bp, bm, bo) = (x, xp, xm, xo), (y, yp, ym, yo)
        st = {}

        def rows_a(k):
            return pl.ds(pl.multiple_of(96 * ((a + k) % 4), 96), 96)

        def s0():
            st["c"], at0 = [], off
            for first, n in ranges:
                mirror = 81 - first - n
                src = gbuf.at[pl.ds(pick(mirror, first), n)]
                st["c"].append(send(src, own.at[pl.ds(at0, n)], sib))
                at0 += n

        def s1():
            for cp in st["c"]:
                cp.wait_recv()
            at0 = off
            for first, n in ranges:
                start = pick(first, 81 - first - n)

                def body(k, carry, start=start, at0=at0):
                    own[at0 + k] = own[at0 + k] + gbuf[start + k]
                    return carry

                lax.fori_loop(0, n, body, 0, unroll=True)
                at0 += n
            st["a"] = [
                send(own.at[mine, rows_a(k)], ra.at[mine, i], device)
                for i, (k, device) in enumerate(((1, ap), (3, am), (2, ao)))
            ]

        def s2():
            for cp in st["a"]:
                cp.wait_recv()
            rows = rows_a(0)

            def block(i):
                v = own[i, rows].astype(F32) + ra[i, 0].astype(F32)
                return v + ra[i, 1].astype(F32) + ra[i, 2].astype(F32)

            at0, p = off, poff
            for _, n in ranges:
                for i in range(at0, at0 + n, 2):
                    one = block(i)
                    two = block(i + 1) if i + 1 < at0 + n else jnp.zeros_like(one)
                    for to in range(4):
                        part = slice(24 * to, 24 * to + 24)
                        sb[to, p] = jnp.concatenate([one[part], two[part]], axis=0).astype(BF)
                    p += 1
                at0 += n
            pairs = pl.ds(poff, p - poff)
            st["q"] = [
                send(sb.at[(b + k) % 4, pairs], q.at[i, pairs], device)
                for i, (k, device) in enumerate(((1, bp), (3, bm), (2, bo)))
            ]

        def s3_():
            for cp in st["q"]:
                cp.wait_recv()
            p, st["owner"] = poff, []
            for first, n in ranges:
                count = (n + 1) // 2
                for i in range(p, p + count):
                    v = sb[b, i].astype(F32) + q[0, i].astype(F32)
                    fin[i] = (v + q[1, i].astype(F32) + q[2, i].astype(F32)).astype(BF)
                mirror = 81 - first - n
                owner = pick(first // 20, (mirror - 10) // 20)
                base = FIXED + 4 * len(to_owner)
                slot, to = (z, 4 * x + y) if order == "xy" else (x, tile)
                cp = pltpu.make_async_remote_copy(
                    src_ref=fin.at[pl.ds(p, count)], dst_ref=fr.at[slot, pl.ds(p, count)],
                    send_sem=send_sem.at[base], recv_sem=recv_sem.at[base + slot],
                    device_id=at(clip=2 * owner + core, tile=to), device_id_type=MESH,
                )
                away = (owner != x) | (to != tile)
                to_owner.append((away, cp))
                st["owner"].append((owner, base, p, n, pick(first % 20, (mirror - 10) % 20)))
                pl.when(away)(cp.start)
                p += count

        def s4():
            for owner, base, p, n, place in st["owner"]:

                @pl.when(owner == x)
                def _(base=base, p=p, n=n, place=place):
                    count = (n + 1) // 2
                    slot = z if order == "xy" else x
                    others = [(slot + k) % 4 for k in (1, 3, 2)]
                    mine = pl.ds(p, count)

                    def arrive(k):
                        pltpu.make_async_remote_copy(
                            src_ref=fin.at[mine], dst_ref=fr.at[k, mine],
                            send_sem=send_sem.at[base], recv_sem=recv_sem.at[base + k],
                            device_id=xp, device_id_type=MESH,
                        ).wait_recv()

                    for k in others:
                        arrive(k)
                    if order == "xy":
                        pl.when(x != z)(lambda: arrive(z))

                        @pl.when(x == z)
                        def _():
                            fr[z, mine] = fin[mine]

                    for i in range(count):
                        v = (fr[z, p + i] if order == "xy" else fin[p + i]).astype(F32)
                        for k in others:
                            v += fr[k, p + i].astype(F32)
                        outf[place + 2 * i] = v[:24]
                        if 2 * i + 1 < n:
                            outf[place + 2 * i + 1] = v[24:]

        return [s0, s1, s2, s3_, s4]

    waves, off, poff = [], 0, 0
    for _, ranges, order in WAVES:
        waves.append(wave_steps(ranges, order, off, poff))
        off += sum(n for _, n in ranges)
        poff += sum((n + 1) // 2 for _, n in ranges)
    orders = {g: order for groups, _, order in WAVES for g in groups}

    def hidden_grad():
        for n in range(0, POS, 256):
            cols = slice(n, n + 256)
            h, inv = hid[:, cols], inv_ref[:, cols]
            normed = h * inv * gain
            s = sigmoid(normed)
            gained = ag[:, cols] * s * (1.0 + normed * (1.0 - s)) * gain
            inner = jnp.mean(gained * h, axis=0, keepdims=True)
            grad = (inv * gained - h * (inv * inv * inv * inner)).astype(BF)
            yt[:, cols] = dot(ink[...], grad, 1, 0)

        col = lax.broadcasted_iota(jnp.int32, (LAT, POS), 1) % W
        summed = []
        for g in range(9):
            base = 48 * g
            after = jnp.where(col == W - 1, 0.0, pltpu.roll(yt[base : base + LAT], POS - 1, 1))
            before = jnp.where(col == 0, 0.0, pltpu.roll(yt[base + 2 * LAT : base + 3 * LAT], 1, 1))
            summed.append(yt[base + LAT : base + 2 * LAT] + after + before)
        for f in range(F):
            for r in range(4):
                total = None
                for dt in range(3):
                    for dy in range(3):
                        fh, rh = f + 2 - dt, r - dy
                        if fh < F and 0 <= rh < R:
                            p = (2 * fh + rh) * W
                            term = summed[3 * dt + dy][:, p : p + W]
                            total = term if total is None else total + term
                lg[f, r, :, 0:W] = total
                lg[f, r, :, W:] = jnp.zeros((LAT, LANES - W), F32)
        pack([lg[f, 0] for f in range(F)], lgs.at[0])
        pack([lg[f, 3] for f in range(F)], lgs.at[1])
        st["lg"] = [send(lgs.at[0], lgr.at[1], tm), send(lgs.at[1], lgr.at[0], tp)]

    def clip_grad():
        for cp in st["lg"]:
            cp.wait_recv()
        tiles = []
        narrow = lax.broadcasted_iota(jnp.int32, (LAT, 128), 1) < 32
        for f in range(F):
            from_up, from_down = (
                jnp.concatenate(
                    [lgr[k, f], jnp.where(narrow, roll(lgr[k, F], -32 * f), 0.0)], axis=1
                )
                for k in range(2)
            )
            first = (lg[f, 1] + from_up * top) * live[f]
            second = (lg[f, 2] + from_down * bottom) * live[f]
            tiles.append(jnp.concatenate([first, second], axis=0))
        pack(tiles, latg2.at[clip])
        st["back"] = [send(latg2.at[clip], latg2.at[clip], d) for d in group]

    def latent_grad():
        for cp in st["back"]:
            cp.wait_recv()
        tiles = [unpack(latg2, route[clip * F + j]) for j in range(F)]
        tr2[...] = jnp.concatenate(tiles, axis=0).T
        for jr in range(8):
            u = jnp.zeros((20, 128), F32)
            for q8 in range(8):
                u = jnp.where(lane16 == q8, roll(tr2[pl.ds(q8, 20, stride=8), :], LAT * (q8 - jr)), u)
            tr1[jr * 24 : jr * 24 + 20] = u
        flat = jnp.concatenate([tr1[pl.ds(g, 8, stride=24), :] for g in range(20)], axis=1)
        for j in range(F):
            out_lat[j] = flat[R * j : R * j + R].astype(BF)

    st = {}
    tail = {"late1": lambda: late_rows(1), "late0": lambda: late_rows(2), "hidden": hidden_grad, "clip": clip_grad, "out": latent_grad}
    for kind, k in SCHEDULE:
        if kind == "G":
            weight_part(k, orders[k])
        elif kind == "A":
            act_grad_part(k // 3, k % 3, False)
        elif kind == "T":
            tail[k]()
        else:
            waves[kind][k]()

    scale = 1.0 / math.sqrt(CLIPS * F * H * W)
    flat = jnp.concatenate([outf[k] * scale for k in range(11)], axis=1)
    out_wg[...] = pltpu.roll(flat, 11 * 128 - 16 * clip, 1)[:, :1296]

    for cp in copies:
        cp.wait_send()
    for away, cp in to_owner:
        pl.when(away)(cp.wait_send)


def hand_out(lat_in, wg_in, lat_out, wg_out):
    lat_out[...] = lat_in[...]
    wg_out[...] = wg_in[...]


def on_device(latents, tile_route, lengths, reward_grad, in_kernel, in_bias, norm_gain, kernel_):
    vmem = pl.BlockSpec(memory_space=pltpu.VMEM)
    smem = pl.BlockSpec(memory_space=pltpu.SMEM)
    hbm = pl.BlockSpec(memory_space=pl.ANY)

    def v(*shape, dtype=BF):
        return pltpu.VMEM(shape, dtype)

    lat_grad, weight_grad = pl.pallas_call(
        kernel,
        out_shape=(
            jax.ShapeDtypeStruct((F, R, W * LAT), BF),
            jax.ShapeDtypeStruct((24, 1296), F32),
        ),
        in_specs=[smem, smem, vmem, hbm, vmem, vmem, vmem, hbm],
        out_specs=(vmem, vmem),
        scratch_shapes=[
            v(F, 4, W, C),
            v(F, 4, W, 3 * C),
            v(27 * C, C),
            v(192, 128, dtype=F32),
            v(LANES, 128, dtype=F32),
            v(F + 1, R * LAT, 128),
            v(CLIPS, F + 1, R * LAT, 128),
            v(F, 4, LAT, LANES),
            v(F, 4, 3 * LAT, LANES),
            v(27 * LAT, POS),
            v(C, POS, dtype=F32),
            v(C, POS),
            v(1, POS, dtype=F32),
            v(C, POS, dtype=F32),
            v(27 * LAT, POS, dtype=F32),
            v(F, 4, LAT, LANES, dtype=F32),
            v(2, F + 1, LAT, 128, dtype=F32),
            v(2, F + 1, LAT, 128, dtype=F32),
            v(CLIPS, F + 1, R * LAT, 128),
            v(81, C, 128),
            v(OWN, C, 128),
            v(OWN, 3, 96, 128),
            v(4, PAIRS, 48, 128),
            v(3, PAIRS, 48, 128),
            v(PAIRS, 48, 128),
            v(4, PAIRS, 48, 128),
            v(11, 24, 128, dtype=F32),
            pltpu.SemaphoreType.DMA((2,)),
            pltpu.SemaphoreType.DMA((FIXED + 36,)),
            pltpu.SemaphoreType.DMA((FIXED + 36,)),
        ],
        compiler_params=pltpu.CompilerParams(
            collective_id=0, has_side_effects=True, vmem_limit_bytes=62 * 2**20
        ),
        name="backward",
    )(
        tile_route, lengths, latents, reward_grad, in_kernel, in_bias, norm_gain, kernel_,
    )
    return pl.pallas_call(
        hand_out,
        out_shape=(
            jax.ShapeDtypeStruct(lat_grad.shape, BF),
            jax.ShapeDtypeStruct(weight_grad.shape, F32),
        ),
        in_specs=[vmem, vmem],
        out_specs=(vmem, vmem),
        name="hand_out",
    )(lat_grad, weight_grad)


def solution(mesh):
    return jax.shard_map(
        on_device,
        mesh=mesh,
        in_specs=(
            P("clip", "tile", None),
            P(),
            P(),
            P("clip", None, "tile", None, None),
            P(),
            P(),
            P(),
            P(),
        ),
        out_specs=(P("clip", "tile", None), P("tile", "clip")),
        check_vma=False,
    )
```

```python
import math

import jax
import jax.numpy as jnp
from jax import lax
from jax.experimental import pallas as pl
from jax.experimental.pallas import tpu as pltpu
from jax.sharding import PartitionSpec as P

EPS = 1e-06
F, R, W, C, LAT, H, CLIPS = 4, 2, 160, 384, 16, 32, 8
POS = F * R * W
LANES = 256
MESH = pl.DeviceIdType.MESH
BF, F32 = jnp.bfloat16, jnp.float32

WAVES = (
    ((1, 7), ((9, 2), (63, 8)), "zy"),
    ((4,), ((40, 5),), "xy"),
    ((0, 8), ((0, 9),), "yz"),
    ((2, 6), ((20, 7), (60, 3)), "zy"),
    ((3, 5), ((27, 4), (45, 6)), "xy"),
)
OWN = 44
FIXED = 80
PAIRS = sum((n + 1) // 2 for _, ranges, _ in WAVES for _, n in ranges)

SCHEDULE = (
    ("G", 1), ("G", 7), (0, 0), ("T", "late1"), ("T", "late0"), ("G", 8), ("G", 0), (2, 0), ("G", 5), (0, 1),
    ("G", 3), (4, 0), ("G", 2), (2, 1), ("G", 6), (3, 0), ("G", 4), (1, 0), (4, 1), ("A", 6), ("A", 3),
    (3, 1), (1, 1), ("A", 8), ("A", 5), ("T", "hidden"), (0, 2), (2, 2), (4, 2), (1, 2), ("T", "clip"),
    (3, 2), (0, 3), (2, 3), (4, 3), (1, 3), (0, 4), (3, 3), (2, 4), ("T", "out"), (1, 4), (4, 4), (3, 4),
)


def dot(a, b, ca, cb):
    return lax.dot_general(a, b, (((ca,), (cb,)), ((), ())), preferred_element_type=F32)


def sigmoid(v):
    return 1.0 / (1.0 + jnp.exp(-v))


def roll(v, shift):
    return pltpu.roll(v, shift % 128, 1) if shift % 128 else v


def pack(tiles, ref):
    rest, dtype = None, ref.dtype
    for f in range(F):
        ref[f] = tiles[f][:, :128].astype(dtype)
        part = roll(tiles[f][:, 128:], 32 * f)
        rest = part if rest is None else rest + part
    ref[F] = rest.astype(dtype)


def unpack(ref, slot):
    owner, j = slot // F, slot % F
    rest = ref[owner, F].astype(F32)
    out = rest
    for k in range(1, F):
        out = jnp.where(j == k, roll(rest, -32 * k), out)
    out = jnp.where(lax.broadcasted_iota(jnp.int32, out.shape, 1) < 32, out, 0.0)
    return jnp.concatenate([ref[owner, j].astype(F32), out], axis=1)


def as_column(ref):
    return jnp.broadcast_to(ref[...].reshape(1, C), (8, C)).T[:, :1]


def kernel(
    route, lengths, lat_in, cot_in, ink, bias_in, gain_in, ker_in,
    out_lat, out_wg,
    cotbuf, cot3, kbuf, tr1, tr2, stage, latg, lat4, s3, xt, hid, act, inv_ref, ag, yt, lg, lgs, lgr, latg2,
    gbuf, own, ra, sb, q, fin, fr, outf,
    local_sem, send_sem, recv_sem,
):
    clip, tile = lax.axis_index("clip"), lax.axis_index("tile")
    x, core = clip // 2, clip % 2
    z, y = tile // 4, tile % 4
    me = {"clip": clip, "tile": tile}

    def at(**kw):
        d = {**me, **kw}
        return (d["clip"], d["tile"])

    sib = at(clip=2 * x + 1 - core)
    xp, xm, xo = (at(clip=2 * ((x + k) % 4) + core) for k in (1, 3, 2))
    others = tuple(at(clip=2 * ((x + k) % 4) + 1 - core) for k in (1, 3, 2))
    group = (xp, xm, xo) + others + (sib,)
    zp, zm, zo = (at(tile=4 * ((z + k) % 4) + y) for k in (1, 3, 2))
    yp, ym, yo = (at(tile=4 * z + (y + k) % 4) for k in (1, 3, 2))
    tp, tm = (at(tile=(tile + k) % 16) for k in (1, 15))
    peers = (sib, xp, xm, xo, zp, zm, zo, yp, ym, yo, tp, tm) + others

    copies = []

    def send(src, dst, device):
        n = len(copies)
        assert n < FIXED
        cp = pltpu.make_async_remote_copy(
            src_ref=src, dst_ref=dst, send_sem=send_sem.at[n], recv_sem=recv_sem.at[n],
            device_id=device, device_id_type=MESH,
        )
        copies.append(cp)
        cp.start()
        return cp

    load_cot = pltpu.make_async_copy(cot_in.at[0], cotbuf.at[:, 1:3], local_sem.at[0])
    load_cot.start()
    load_ker = pltpu.make_async_copy(ker_in, kbuf, local_sem.at[1])
    load_ker.start()

    barrier = pltpu.get_barrier_semaphore()
    for p in peers:
        pl.semaphore_signal(barrier, inc=1, device_id=p, device_id_type=MESH)
    def greet(p):
        pl.semaphore_signal(barrier, inc=1, device_id=p, device_id_type=MESH)

    for k in (1, 2, 3):
        greet(at(clip=2 * z + core, tile=4 * ((z + k) % 4) + y))
    pl.when(x != z)(lambda: greet(at(clip=2 * z + core, tile=4 * z + y)))

    lane16 = lax.broadcasted_iota(jnp.int32, (20, 128), 1) // LAT
    flat = jnp.concatenate([lat_in[j].astype(F32) for j in range(F)], axis=0)
    for g in range(20):
        tr1[pl.ds(g, 8, stride=24), :] = flat[:, 128 * g : 128 * (g + 1)]
    tr2[W:] = jnp.zeros((LANES - W, 128), F32)
    for q8 in range(8):
        u = jnp.zeros((20, 128), F32)
        for jr in range(8):
            u = jnp.where(lane16 == jr, roll(tr1[jr * 24 : jr * 24 + 20], LAT * (jr - q8)), u)
        tr2[pl.ds(q8, 20, stride=8), :] = u
    pack(tr2[...].T.reshape(F, R * LAT, LANES), stage)

    pl.semaphore_wait(barrier, len(peers) + 3 + jnp.where(x != z, 1, 0))

    lat_g = [send(stage, latg.at[clip], d) for d in group]
    parts = (slice(2, 4), slice(1, 2), slice(0, 1))
    halo = [
        [
            send(cot_in.at[0, part, 0], cotbuf.at[part, 3], tm),
            send(cot_in.at[0, part, 1], cotbuf.at[part, 0], tp),
        ]
        for part in parts
    ]
    latg[clip] = stage[...]

    length = lengths[clip]
    live = [jnp.where(f < length, 1.0, 0.0).astype(F32) for f in range(F)]
    top = jnp.where(tile > 0, 1.0, 0.0).astype(F32)
    bottom = jnp.where(tile < 15, 1.0, 0.0).astype(F32)
    edge = (top, 1.0, 1.0, bottom)

    def build_cot(rows, frames):
        col = lax.broadcasted_iota(jnp.int32, (W, C), 0)
        for f in frames:
            for r in rows:
                v = cotbuf[f, r].astype(F32) * (live[f] * edge[r])
                after = jnp.where(col == W - 1, 0.0, pltpu.roll(v, W - 1, 0))
                before = jnp.where(col == 0, 0.0, pltpu.roll(v, 1, 0))
                cot3[f, r, :, 0:C] = after.astype(BF)
                cot3[f, r, :, C : 2 * C] = v.astype(BF)
                cot3[f, r, :, 2 * C : 3 * C] = before.astype(BF)

    def window(dt, dy):
        return cot3[2 - dt : 4, 2 - dy : 4 - dy].reshape((dt + 2) * R * W, 3 * C)

    def act_grad_part(dt, dy, first):
        t0 = 9 * dt + 3 * dy
        taps = jnp.concatenate([kbuf[(t0 + d) * C : (t0 + d + 1) * C] for d in range(3)], axis=1)
        out = dot(taps, window(dt, dy), 1, 1)
        n = (dt + 2) * R * W
        if first:
            ag[...] = out
        else:
            ag[:, :n] += out

    def late_rows(k):
        for cp in halo[k]:
            cp.wait_recv()
        build_cot((0, 3), range(F)[parts[k]])

    load_cot.wait()
    build_cot((1, 2), range(F))

    load_ker.wait()
    act_grad_part(2, 1, True)
    act_grad_part(1, 1, False)
    act_grad_part(0, 1, False)
    for cp in lat_g:
        cp.wait_recv()

    for f in range(F):
        slot = jnp.int32(0)
        for s in range(CLIPS * F):
            slot = jnp.where(route[s] == clip * F + f, s, slot)
        v = unpack(latg, slot) * live[f]
        lat4[f, 1] = v[:LAT].astype(BF)
        lat4[f, 2] = v[LAT:].astype(BF)
    lat_h = [send(lat4.at[:, 1], lat4.at[:, 3], tm), send(lat4.at[:, 2], lat4.at[:, 0], tp)]
    late_rows(0)
    act_grad_part(0, 0, False)
    act_grad_part(0, 2, False)
    for cp in lat_h:
        cp.wait_recv()

    for f in range(F):
        for r in range(4):
            v = lat4[f, r].astype(F32) * edge[r]
            s3[f, r, 0:LAT] = pltpu.roll(v, 1, 1).astype(BF)
            s3[f, r, LAT : 2 * LAT] = v.astype(BF)
            s3[f, r, 2 * LAT :] = pltpu.roll(v, LANES - 1, 1).astype(BF)
    for f in range(F):
        for r in range(R):
            for dt in range(3):
                for dy in range(3):
                    at_rows = slice((3 * dt + dy) * 48, (3 * dt + dy + 1) * 48)
                    at_cols = slice((2 * f + r) * W, (2 * f + r + 1) * W)
                    if f - 2 + dt >= 0:
                        xt[at_rows, at_cols] = s3[f - 2 + dt, r + dy, :, 0:W]
                    else:
                        xt[at_rows, at_cols] = jnp.zeros((48, W), BF)
    gain = as_column(gain_in)
    bias = as_column(bias_in)
    for n in range(0, POS, 256):
        cols = slice(n, n + 256)
        h = dot(ink[...], xt[:, cols], 0, 0) + bias
        hid[:, cols] = h
        inv = lax.rsqrt(jnp.mean(h * h, axis=0, keepdims=True) + EPS)
        normed = h * inv * gain
        act[:, cols] = (normed * sigmoid(normed)).astype(BF)
        inv_ref[:, cols] = inv

    def weight_part(g, order):
        dt, dy = g // 3, g % 3
        out = dot(act[:, : (dt + 2) * R * W], window(dt, dy), 1, 0)
        for k in range(9):
            v = out[:, 128 * k : 128 * (k + 1)]
            if order == "yz":
                v = jnp.concatenate(
                    [v[24 * (4 * b + a) : 24 * (4 * b + a) + 24] for a in range(4) for b in range(4)], axis=0
                )
            gbuf[9 * g + k] = v.astype(BF)

    def pick(a, b):
        return jnp.where(core == 0, a, b)

    to_owner = []

    def wave_steps(ranges, order, off, poff):
        total = sum(n for _, n in ranges)
        mine = pl.ds(off, total)
        if order == "zy":
            (a, ap, am, ao), (b, bp, bm, bo) = (z, zp, zm, zo), (y, yp, ym, yo)
        elif order == "yz":
            (a, ap, am, ao), (b, bp, bm, bo) = (y, yp, ym, yo), (z, zp, zm, zo)
        else:
            (a, ap, am, ao), (b, bp, bm, bo) = (x, xp, xm, xo), (y, yp, ym, yo)
        st = {}

        def rows_a(k):
            return pl.ds(pl.multiple_of(96 * ((a + k) % 4), 96), 96)

        def s0():
            st["c"], at0 = [], off
            for first, n in ranges:
                mirror = 81 - first - n
                src = gbuf.at[pl.ds(pick(mirror, first), n)]
                st["c"].append(send(src, own.at[pl.ds(at0, n)], sib))
                at0 += n

        def s1():
            for cp in st["c"]:
                cp.wait_recv()
            at0 = off
            for first, n in ranges:
                start = pick(first, 81 - first - n)

                def body(k, carry, start=start, at0=at0):
                    own[at0 + k] = own[at0 + k] + gbuf[start + k]
                    return carry

                lax.fori_loop(0, n, body, 0, unroll=True)
                at0 += n
            st["a"] = [
                send(own.at[mine, rows_a(k)], ra.at[mine, i], device)
                for i, (k, device) in enumerate(((1, ap), (3, am), (2, ao)))
            ]

        def s2():
            for cp in st["a"]:
                cp.wait_recv()
            rows = rows_a(0)

            def block(i):
                v = own[i, rows].astype(F32) + ra[i, 0].astype(F32)
                return v + ra[i, 1].astype(F32) + ra[i, 2].astype(F32)

            at0, p = off, poff
            for _, n in ranges:
                for i in range(at0, at0 + n, 2):
                    one = block(i)
                    two = block(i + 1) if i + 1 < at0 + n else jnp.zeros_like(one)
                    for to in range(4):
                        part = slice(24 * to, 24 * to + 24)
                        sb[to, p] = jnp.concatenate([one[part], two[part]], axis=0).astype(BF)
                    p += 1
                at0 += n
            pairs = pl.ds(poff, p - poff)
            st["q"] = [
                send(sb.at[(b + k) % 4, pairs], q.at[i, pairs], device)
                for i, (k, device) in enumerate(((1, bp), (3, bm), (2, bo)))
            ]

        def s3_():
            for cp in st["q"]:
                cp.wait_recv()
            p, st["owner"] = poff, []
            for first, n in ranges:
                count = (n + 1) // 2
                for i in range(p, p + count):
                    v = sb[b, i].astype(F32) + q[0, i].astype(F32)
                    fin[i] = (v + q[1, i].astype(F32) + q[2, i].astype(F32)).astype(BF)
                mirror = 81 - first - n
                owner = pick(first // 20, (mirror - 10) // 20)
                base = FIXED + 4 * len(to_owner)
                slot, to = (z, 4 * x + y) if order == "xy" else (x, tile)
                cp = pltpu.make_async_remote_copy(
                    src_ref=fin.at[pl.ds(p, count)], dst_ref=fr.at[slot, pl.ds(p, count)],
                    send_sem=send_sem.at[base], recv_sem=recv_sem.at[base + slot],
                    device_id=at(clip=2 * owner + core, tile=to), device_id_type=MESH,
                )
                away = (owner != x) | (to != tile)
                to_owner.append((away, cp))
                st["owner"].append((owner, base, p, n, pick(first % 20, (mirror - 10) % 20)))
                pl.when(away)(cp.start)
                p += count

        def s4():
            for owner, base, p, n, place in st["owner"]:

                @pl.when(owner == x)
                def _(base=base, p=p, n=n, place=place):
                    count = (n + 1) // 2
                    slot = z if order == "xy" else x
                    others = [(slot + k) % 4 for k in (1, 3, 2)]
                    mine = pl.ds(p, count)

                    def arrive(k):
                        pltpu.make_async_remote_copy(
                            src_ref=fin.at[mine], dst_ref=fr.at[k, mine],
                            send_sem=send_sem.at[base], recv_sem=recv_sem.at[base + k],
                            device_id=xp, device_id_type=MESH,
                        ).wait_recv()

                    for k in others:
                        arrive(k)
                    if order == "xy":
                        pl.when(x != z)(lambda: arrive(z))

                        @pl.when(x == z)
                        def _():
                            fr[z, mine] = fin[mine]

                    for i in range(count):
                        v = (fr[z, p + i] if order == "xy" else fin[p + i]).astype(F32)
                        for k in others:
                            v += fr[k, p + i].astype(F32)
                        outf[place + 2 * i] = v[:24]
                        if 2 * i + 1 < n:
                            outf[place + 2 * i + 1] = v[24:]

        return [s0, s1, s2, s3_, s4]

    waves, off, poff = [], 0, 0
    for _, ranges, order in WAVES:
        waves.append(wave_steps(ranges, order, off, poff))
        off += sum(n for _, n in ranges)
        poff += sum((n + 1) // 2 for _, n in ranges)
    orders = {g: order for groups, _, order in WAVES for g in groups}

    def hidden_grad():
        for n in range(0, POS, 256):
            cols = slice(n, n + 256)
            h, inv = hid[:, cols], inv_ref[:, cols]
            normed = h * inv * gain
            s = sigmoid(normed)
            gained = ag[:, cols] * s * (1.0 + normed * (1.0 - s)) * gain
            inner = jnp.mean(gained * h, axis=0, keepdims=True)
            grad = (inv * gained - h * (inv * inv * inv * inner)).astype(BF)
            yt[:, cols] = dot(ink[...], grad, 1, 0)

        col = lax.broadcasted_iota(jnp.int32, (LAT, POS), 1) % W
        summed = []
        for g in range(9):
            base = 48 * g
            after = jnp.where(col == W - 1, 0.0, pltpu.roll(yt[base : base + LAT], POS - 1, 1))
            before = jnp.where(col == 0, 0.0, pltpu.roll(yt[base + 2 * LAT : base + 3 * LAT], 1, 1))
            summed.append(yt[base + LAT : base + 2 * LAT] + after + before)
        for f in range(F):
            for r in range(4):
                total = None
                for dt in range(3):
                    for dy in range(3):
                        fh, rh = f + 2 - dt, r - dy
                        if fh < F and 0 <= rh < R:
                            p = (2 * fh + rh) * W
                            term = summed[3 * dt + dy][:, p : p + W]
                            total = term if total is None else total + term
                lg[f, r, :, 0:W] = total
                lg[f, r, :, W:] = jnp.zeros((LAT, LANES - W), F32)
        pack([lg[f, 0] for f in range(F)], lgs.at[0])
        pack([lg[f, 3] for f in range(F)], lgs.at[1])
        st["lg"] = [send(lgs.at[0], lgr.at[1], tm), send(lgs.at[1], lgr.at[0], tp)]

    def clip_grad():
        for cp in st["lg"]:
            cp.wait_recv()
        tiles = []
        narrow = lax.broadcasted_iota(jnp.int32, (LAT, 128), 1) < 32
        for f in range(F):
            from_up, from_down = (
                jnp.concatenate(
                    [lgr[k, f], jnp.where(narrow, roll(lgr[k, F], -32 * f), 0.0)], axis=1
                )
                for k in range(2)
            )
            first = (lg[f, 1] + from_up * top) * live[f]
            second = (lg[f, 2] + from_down * bottom) * live[f]
            tiles.append(jnp.concatenate([first, second], axis=0))
        pack(tiles, latg2.at[clip])
        st["back"] = [send(latg2.at[clip], latg2.at[clip], d) for d in group]

    def latent_grad():
        for cp in st["back"]:
            cp.wait_recv()
        tiles = [unpack(latg2, route[clip * F + j]) for j in range(F)]
        tr2[...] = jnp.concatenate(tiles, axis=0).T
        for jr in range(8):
            u = jnp.zeros((20, 128), F32)
            for q8 in range(8):
                u = jnp.where(lane16 == q8, roll(tr2[pl.ds(q8, 20, stride=8), :], LAT * (q8 - jr)), u)
            tr1[jr * 24 : jr * 24 + 20] = u
        flat = jnp.concatenate([tr1[pl.ds(g, 8, stride=24), :] for g in range(20)], axis=1)
        for j in range(F):
            out_lat[j] = flat[R * j : R * j + R].astype(BF)

    st = {}
    tail = {"late1": lambda: late_rows(1), "late0": lambda: late_rows(2), "hidden": hidden_grad, "clip": clip_grad, "out": latent_grad}
    for kind, k in SCHEDULE:
        if kind == "G":
            weight_part(k, orders[k])
        elif kind == "A":
            act_grad_part(k // 3, k % 3, False)
        elif kind == "T":
            tail[k]()
        else:
            waves[kind][k]()

    scale = 1.0 / math.sqrt(CLIPS * F * H * W)
    flat = jnp.concatenate([outf[k] * scale for k in range(11)], axis=1)
    out_wg[...] = pltpu.roll(flat, 11 * 128 - 16 * clip, 1)[:, :1296]

    for cp in copies:
        cp.wait_send()
    for away, cp in to_owner:
        pl.when(away)(cp.wait_send)


def hand_out(lat_in, wg_in, lat_out, wg_out):
    lat_out[...] = lat_in[...]
    wg_out[...] = wg_in[...]


def on_device(latents, tile_route, lengths, reward_grad, in_kernel, in_bias, norm_gain, kernel_):
    vmem = pl.BlockSpec(memory_space=pltpu.VMEM)
    smem = pl.BlockSpec(memory_space=pltpu.SMEM)
    hbm = pl.BlockSpec(memory_space=pl.ANY)

    def v(*shape, dtype=BF):
        return pltpu.VMEM(shape, dtype)

    lat_grad, weight_grad = pl.pallas_call(
        kernel,
        out_shape=(
            jax.ShapeDtypeStruct((F, R, W * LAT), BF),
            jax.ShapeDtypeStruct((24, 1296), F32),
        ),
        in_specs=[smem, smem, vmem, hbm, vmem, vmem, vmem, hbm],
        out_specs=(vmem, vmem),
        scratch_shapes=[
            v(F, 4, W, C),
            v(F, 4, W, 3 * C),
            v(27 * C, C),
            v(192, 128, dtype=F32),
            v(LANES, 128, dtype=F32),
            v(F + 1, R * LAT, 128),
            v(CLIPS, F + 1, R * LAT, 128),
            v(F, 4, LAT, LANES),
            v(F, 4, 3 * LAT, LANES),
            v(27 * LAT, POS),
            v(C, POS, dtype=F32),
            v(C, POS),
            v(1, POS, dtype=F32),
            v(C, POS, dtype=F32),
            v(27 * LAT, POS, dtype=F32),
            v(F, 4, LAT, LANES, dtype=F32),
            v(2, F + 1, LAT, 128, dtype=F32),
            v(2, F + 1, LAT, 128, dtype=F32),
            v(CLIPS, F + 1, R * LAT, 128),
            v(81, C, 128),
            v(OWN, C, 128),
            v(OWN, 3, 96, 128),
            v(4, PAIRS, 48, 128),
            v(3, PAIRS, 48, 128),
            v(PAIRS, 48, 128),
            v(4, PAIRS, 48, 128),
            v(11, 24, 128, dtype=F32),
            pltpu.SemaphoreType.DMA((2,)),
            pltpu.SemaphoreType.DMA((FIXED + 36,)),
            pltpu.SemaphoreType.DMA((FIXED + 36,)),
        ],
        compiler_params=pltpu.CompilerParams(
            collective_id=0, has_side_effects=True, vmem_limit_bytes=62 * 2**20
        ),
        name="backward",
    )(
        tile_route, lengths, latents, reward_grad, in_kernel, in_bias, norm_gain, kernel_,
    )
    return pl.pallas_call(
        hand_out,
        out_shape=(
            jax.ShapeDtypeStruct(lat_grad.shape, BF),
            jax.ShapeDtypeStruct(weight_grad.shape, F32),
        ),
        in_specs=[vmem, vmem],
        out_specs=(vmem, vmem),
        name="hand_out",
    )(lat_grad, weight_grad)


def solution(mesh):
    return jax.shard_map(
        on_device,
        mesh=mesh,
        in_specs=(
            P("clip", "tile", None),
            P(),
            P(),
            P("clip", None, "tile", None, None),
            P(),
            P(),
            P(),
            P(),
        ),
        out_specs=(P("clip", "tile", None), P("tile", "clip")),
        check_vma=False,
    )
```
